256 devices in a mesh: seq: 16 (over y, z_lo, core), row: 4 (over z_hi), col: 4 (over x).
Axes of the slice: x: 4, y: 4, z: 8 (z_hi: 4, z_lo: 2; z = z_hi * 2 + z_lo), core: 2. Of those that a mesh axis runs over, the one named last changes fastest.
Arguments:
- tokens: bfloat16 [8192, 4096], P(('seq', 'row'), 'col'), may hold values from -6 to 6
- w_uvqk: bfloat16 [4096, 8192], P(('seq', 'row'), 'col'), may hold values from -0.09375 to 0.09375
- w_out: bfloat16 [2048, 4096], P('col', ('seq', 'row')), may hold values from -0.375 to 0.375
- rab_table: float32 [16, 32], replicated, may hold values from -4 to 4
- norm_gain: float32 [16, 128], replicated, may hold values from 0.5 to 2
- user_lengths: int32 [4], replicated, may hold values from 1 to 6144, 8192 in all
- bucket_ids: int32 [8192], P('seq'), may hold values from 0 to 8191, as said below
Outputs:
- layer_out: bfloat16 [8192, 4096], P(('seq', 'row'), 'col')
The draws below stay inside these ranges and needn't reach their ends.
Inputs may be any that keep to these rules, and one draw needn't show every extreme that they name: bucket_ids never fall from one token to the next.
All inputs are finite; a program needn't handle non-finite values.
Results may differ from the reference program's by a relative error of at most 0.014.
Values may be sent and summed in bfloat16 or wider, within the bound.
No kernel may reach another device: no remote copies, remote signals or barrier semaphores. Data moves between devices by JAX's collectives and lax.ppermute only.
A program may use at most 64 MiB of HBM per device.

```python
import math
import jax
import jax.numpy as jnp
import numpy as np
from jax import lax

D = 4096
HEADS = 16
DH = 128
NB = 32
USERS = 4
TOKENS = 8192
HD = 2048
MAXLEN = 6144


def draw_bucket_ids(key, part):
    key = jax.random.fold_in(key, 7)
    increments = jax.random.randint(key, (TOKENS,), 1, 3, dtype=jnp.int32)
    increments = increments.at[0].set(0)
    return jnp.minimum(jnp.cumsum(increments), TOKENS - 1).astype(jnp.int32)


def raised(values, stream_key, source, target, shards_of, factor):
    owner, partner = [(jnp.arange(values.shape[axis_at]) // (values.shape[axis_at] // shards_of)).reshape([-1 if axis == axis_at else 1 for axis in range(values.ndim)]) for axis_at in (source, target)]
    chosen = jax.random.permutation(stream_key, shards_of)[partner]
    strong = (owner == chosen) | (owner == (partner + shards_of // 2) % shards_of)
    return jnp.where(strong, factor * values, values)


def shard_levels(own_key, extent, shards, low, high):
    loudness, own = 1.0, jax.random.fold_in(own_key, 6)
    for dim, parts in shards:
        heights = jnp.exp(jax.random.uniform(jax.random.fold_in(own, dim), (parts,), jnp.float32, low / len(shards), high / len(shards)))
        loudness = loudness * jnp.repeat(heights, extent[dim] // parts).reshape([-1 if axis == dim else 1 for axis in range(len(extent))])
    return loudness


def split_up(number_of, total, limit, lean):
    loads = [(1 << 20) // math.isqrt(rank ** lean) + 1 for rank in range(2, number_of + 1)]
    rest, holding = total - limit - (number_of - 1), [1] * (number_of - 1)
    while rest > 0:
        candidates = [i for i in range(number_of - 1) if holding[i] < limit]
        pool, remaining = sum([loads[i] for i in candidates]), rest
        for i in candidates:
            extra = min(limit - holding[i], max(1, remaining * loads[i] // pool), rest)
            holding[i] = holding[i] + extra
            rest = rest - extra
    return np.array([limit] + holding)


def uneven(key, count, total, limit, skew):
    if count == 2:
        one = jax.random.randint(key, (), max(1, total - limit), min(limit, total - 1) + 1)
        return jnp.stack([one, total - one])
    lengths = jnp.asarray(split_up(count, total, limit, skew), jnp.int32)
    couples = (count - 1) // 2
    source_of, receiver = lengths[1:1 + 2 * couples:2], lengths[2:2 + 2 * couples:2]
    room = jnp.minimum(source_of - 1, limit - receiver)
    shifted = jax.random.randint(jax.random.fold_in(key, 1), (couples,), 0, 1 << 20) % (room + 1)
    lengths = lengths.at[1:1 + 2 * couples:2].set(source_of - shifted).at[2:2 + 2 * couples:2].set(receiver + shifted)
    return lengths[jax.random.permutation(jax.random.fold_in(key, 2), count)]


def bell_draw(stream_key, shape, scale, limit, pieces=(), kind=jnp.bfloat16):
    level = shard_levels(stream_key, shape, pieces, -0.22, 0.18) if pieces else 1.0
    result = jax.random.normal(stream_key, shape, jnp.float32) * scale * level
    return jnp.minimum(jnp.maximum(result, -limit), limit).astype(kind)


def bell_draw_with(rng, extent, scale, limit, split, heavy, held_as=jnp.bfloat16):
    array = scale * jax.random.normal(rng, extent, jnp.float32)
    if split:
        array = array * shard_levels(rng, extent, split, -0.22, 0.18)
    return jnp.clip(raised(array, jax.random.fold_in(rng, 3), *heavy), -limit, limit).astype(held_as)


def setup_inputs(seed: int = 0) -> dict:
    key_list = jax.random.split(jax.random.key(seed), 8)
    tokens = bell_draw(key_list[0], (TOKENS, D), 1.0, 6.0, ((0, 64), (1, 4)))
    w_uvqk = bell_draw(key_list[1], (D, 4 * HD), D ** -0.5, 0.09375, ((0, 64), (1, 4)))
    w_out = bell_draw_with(key_list[2], (HD, D), HD ** -0.5, 0.375, ((0, 4), (1, 64)), (0, 1, 64, 4.0))
    rab_table = bell_draw(key_list[3], (HEADS, NB), 1.0, 4.0, (), jnp.float32)
    norm_gain = jnp.clip(jax.random.uniform(key_list[4], (HEADS, DH), jnp.float32, 0.5, 2.0), 0.5, 2.0)
    user_lengths = uneven(key_list[5], USERS, TOKENS, MAXLEN, 2).astype(jnp.int32)
    bucket_ids = draw_bucket_ids(jax.random.fold_in(key_list[7], 71), 0)
    return {"tokens": tokens, "w_uvqk": w_uvqk, "w_out": w_out, "rab_table": rab_table, "norm_gain": norm_gain, "user_lengths": user_lengths, "bucket_ids": bucket_ids}


norm_eps = 1e-05

def user_index(user_ends, positions):
    return lax.optimization_barrier(jnp.sum((user_ends[None, :] <= positions[:, None]).astype(jnp.int32), axis=1)).astype(jnp.int32)

def bucket_bias(table_row, bucket_gap):
    bias_sum = jnp.zeros(bucket_gap.shape, jnp.float32)
    for bucket_no in range(NB):
        bias_sum = bias_sum + jnp.where(bucket_gap == bucket_no, table_row[bucket_no], jnp.float32(0.0))
    return bias_sum

def reference(tokens, w_uvqk, w_out, rab_table, norm_gain, user_lengths, bucket_ids):
    projected = jnp.dot(tokens, w_uvqk, preferred_element_type=jnp.float32)
    activated = jax.nn.silu(projected).astype(jnp.bfloat16).reshape(TOKENS, HEADS, 4, DH)
    positions = jnp.arange(TOKENS, dtype=jnp.int32)
    user_ends = jnp.cumsum(user_lengths).astype(jnp.int32)
    users = user_index(user_ends, positions)
    block_size = math.gcd(TOKENS, 1024)
    block_count = TOKENS // block_size
    score_scale = DH ** (-0.5)

    def one_head(head_args):
        head_uvqk, rab_row, gain_row = head_args
        key_rows = head_uvqk[:, 3]
        values = head_uvqk[:, 1]
        queries = head_uvqk[:, 2]

        def one_block(block_no):
            first_row = (block_no * block_size).astype(jnp.int32)
            query_rows = lax.dynamic_slice_in_dim(queries, first_row, block_size, 0)
            query_pos = first_row + jnp.arange(block_size, dtype=jnp.int32)
            query_user = lax.dynamic_slice_in_dim(users, first_row, block_size, 0)
            query_bucket = lax.dynamic_slice_in_dim(bucket_ids, first_row, block_size, 0)
            bucket_gap = jnp.clip(query_bucket[:, None] - bucket_ids[None, :], 0, NB - 1)
            scores = jnp.dot(query_rows, key_rows.T, preferred_element_type=jnp.float32) * score_scale
            scores = scores + bucket_bias(rab_row, bucket_gap)
            visible = (query_user[:, None] == users[None, :]) & (positions[None, :] <= query_pos[:, None])
            weights = jnp.where(visible, jax.nn.silu(scores), jnp.float32(0.0)).astype(jnp.bfloat16)
            return jnp.dot(weights, values, preferred_element_type=jnp.float32)
        attended = lax.map(one_block, jnp.arange(block_count, dtype=jnp.int32)).reshape(TOKENS, DH)
        head_mean = lax.optimization_barrier(jnp.mean(attended, axis=-1, keepdims=True))
        centered = attended - head_mean
        head_var = lax.optimization_barrier(jnp.mean(centered * centered, axis=-1, keepdims=True))
        normed = centered * lax.rsqrt(head_var + norm_eps) * gain_row[None, :]
        return (normed * head_uvqk[:, 0].astype(jnp.float32)).astype(jnp.bfloat16)
    gated = lax.map(one_head, (jnp.moveaxis(activated, 1, 0), rab_table, norm_gain))
    gated = jnp.moveaxis(gated, 0, 1).reshape(TOKENS, HEADS * DH)
    layer_out = tokens.astype(jnp.float32) + jnp.dot(gated, w_out, preferred_element_type=jnp.float32)
    return layer_out.astype(jnp.bfloat16)
```

```python
import functools

import jax
import jax.numpy as jnp
from jax import lax
from jax.experimental import pallas as pl
from jax.experimental.pallas import tpu as pltpu
from jax.sharding import Mesh
from jax.sharding import PartitionSpec as P

DH = 128
NB = 32
RUN = 128
TILE = 512
NORM_EPS = 1e-05
SCALE = DH ** (-0.5)


def rotations(value, axis, size, step=1):
    return [value] + [
        lax.ppermute(value, axis, [(i, (i + step * k) % size) for i in range(size)])
        for k in range(1, size)
    ]


def z_shift(k):
    pairs = []
    for zl in range(2):
        for zh in range(4):
            to = (zh * 2 + zl + k) % 8
            pairs.append((zl * 4 + zh, (to % 2) * 4 + to // 2))
    return pairs


def project_kernel(place, t0, t1, t2, t3, mine, other, kv_ref, uq_ref, sorted_w, total):
    y, zl, core, zh, x = (place[i] for i in range(5))
    z = zh * 2 + zl
    for kx, chunk in enumerate((t0, t1, t2, t3)):
        ky = (y - (x - kx)) & 3
        for kz in range(8):
            z_from = (z - kz) & 7
            for c, source in enumerate((mine, other)):
                core_from = core if c == 0 else 1 - core
                piece = ((z_from & 1) * 2 + core_from) * 4 + (z_from >> 1)
                rows = pl.ds(pl.multiple_of(piece * 64, 64), 64)
                sorted_w[rows, :] = source[kz, ky]
        part = jnp.dot(chunk[...], sorted_w[...], preferred_element_type=jnp.float32)
        if kx == 0:
            total[...] = part
        else:
            total[...] += part
    half = 0.5 * total[...]
    act = (half + half * jnp.tanh(half)).astype(jnp.bfloat16)
    for r in range(4):
        rows = slice(r * RUN, (r + 1) * RUN)
        uq_ref[r, :, :DH] = act[rows, :DH]
        kv_ref[r, :, :DH] = act[rows, DH : 2 * DH]
        uq_ref[r, :, DH:] = act[rows, 2 * DH : 3 * DH]
        kv_ref[r, :, DH:] = act[rows, 3 * DH :]


def attend_kernel(
    place, lengths, q_edges, k_edges, biases, kv_ref, uq_ref, q_ids, k_ids, table, gain, out_ref, acc
):
    y, zl, core, zh = (place[i] for i in range(4))
    block = zl * 2 + core
    end0 = lengths[0]
    end1 = end0 + lengths[1]
    end2 = end1 + lengths[2]

    def user_start(pos):
        return jnp.where(pos >= end2, end2, jnp.where(pos >= end1, end1, jnp.where(pos >= end0, end0, 0)))

    table_rows = jnp.broadcast_to(table[...], (RUN, DH))
    for r in range(4):
        run_tile = ((y - r) & 3) * 4 + block
        first = run_tile * TILE + zh * RUN
        low_first, low_last = user_start(first), user_start(first + RUN - 1)
        queries = uq_ref[r, :, DH:]
        q_low, q_high = q_edges[r, 0], q_edges[r, 1]
        acc[...] = jnp.zeros_like(acc)

        def tile(kt, carry):
            ky, km = (y - (kt >> 2)) & 3, kt & 3
            pieces = pl.ds(km * 4, 4)
            keys = kv_ref[pieces, ky, :, DH:].reshape(TILE, DH)
            values = kv_ref[pieces, ky, :, :DH].reshape(TILE, DH)
            entry = ky * 4 + km
            gap_low = jnp.clip(q_low - k_edges[entry, 1], 0, NB - 1)
            gap_high = jnp.clip(q_high - k_edges[entry, 0], 0, NB - 1)
            plain = (kt < run_tile) & (kt * TILE >= low_last) & (gap_low == gap_high)
            scores = lax.dot_general(
                queries, keys, (((1,), (1,)), ((), ())), preferred_element_type=jnp.float32
            ) * (0.5 * SCALE)

            @pl.when(plain)
            def _():
                half = scores + 0.5 * biases[gap_low]
                weights = (half + half * jnp.tanh(half)).astype(jnp.bfloat16)
                acc[...] += jnp.dot(weights, values, preferred_element_type=jnp.float32)

            @pl.when(jnp.logical_not(plain))
            def _():
                gaps = jnp.clip(q_ids[r] - k_ids[ky, pl.ds(km, 1), :], 0, NB - 1)
                bias = jnp.concatenate(
                    [
                        jnp.take_along_axis(
                            table_rows,
                            gaps[:, c * DH : (c + 1) * DH],
                            axis=1,
                            mode="promise_in_bounds",
                        )
                        for c in range(TILE // DH)
                    ],
                    axis=1,
                )
                half = scores + 0.5 * bias
                silu = half + half * jnp.tanh(half)
                q_pos = first + lax.broadcasted_iota(jnp.int32, (RUN, TILE), 0)
                k_pos = kt * TILE + lax.broadcasted_iota(jnp.int32, (RUN, TILE), 1)
                seen = (k_pos <= q_pos) & (k_pos >= user_start(q_pos))
                weights = jnp.where(seen, silu, 0.0).astype(jnp.bfloat16)
                acc[...] += jnp.dot(weights, values, preferred_element_type=jnp.float32)

            return carry

        lax.fori_loop(low_first // TILE, run_tile + 1, tile, 0)
        attended = acc[...]
        mean = jnp.mean(attended, axis=-1, keepdims=True)
        centered = attended - mean
        var = jnp.mean(centered * centered, axis=-1, keepdims=True)
        normed = centered * lax.rsqrt(var + NORM_EPS) * gain[...]
        out_ref[r] = (normed * uq_ref[r, :, :DH].astype(jnp.float32)).astype(jnp.bfloat16)


def output_kernel(place, tokens, gated, w0, w1, w2, w3, out_ref, rows):
    y, x = place[0], place[4]
    for kx in range(4):
        for k in range(4):
            head = ((x - kx) & 3) * 4 + ((y + k) & 3)
            rows[:, pl.ds(pl.multiple_of(head * DH, DH), DH)] = gated[kx, :, k * DH : (k + 1) * DH]
    total = tokens[...].astype(jnp.float32)
    for ky, weight in enumerate((w0, w1, w2, w3)):
        source = (y - ky) & 3
        left = rows[:, pl.ds(pl.multiple_of(source * 512, 512), 512)]
        total += lax.dot_general(
            left, weight[...].reshape(1024, 512), (((1,), (1,)), ((), ())), preferred_element_type=jnp.float32
        )
    out_ref[...] = total.astype(jnp.bfloat16)


def call(kernel, shapes, n_smem, n_vmem, scratch, flops, moved, name):
    return pl.pallas_call(
        kernel,
        out_shape=shapes,
        in_specs=[pl.BlockSpec(memory_space=pltpu.SMEM)] * n_smem
        + [pl.BlockSpec(memory_space=pltpu.VMEM)] * n_vmem,
        out_specs=jax.tree.map(lambda _: pl.BlockSpec(memory_space=pltpu.VMEM), shapes),
        scratch_shapes=scratch,
        compiler_params=pltpu.CompilerParams(vmem_limit_bytes=40 * 2**20),
        cost_estimate=pl.CostEstimate(flops=flops, bytes_accessed=moved, transcendentals=0),
        name=name,
    )


def on_device(tokens, w_uvqk, w_out, rab_table, norm_gain, user_lengths, bucket_ids):
    bf16 = jnp.bfloat16
    y, zl, core, zh, x = (lax.axis_index(a) for a in ("y", "zl", "core", "zh", "x"))
    place = jnp.stack([y, zl, core, zh, x]).astype(jnp.int32)
    plane = ("zl", "core", "zh")

    swapped = lax.ppermute(w_out.T, ("y", "x"), [(b * 4 + a, a * 4 + b) for a in range(4) for b in range(4)])
    ids = jnp.stack([bucket_ids // 128, bucket_ids % 128]).astype(bf16)
    ids = jnp.concatenate(rotations(ids, "y", 4) + [jnp.zeros((8, TILE), bf16)], axis=0)
    wo_and_ids = lax.all_gather(jnp.concatenate([swapped, ids], axis=0), plane)

    def columns(owner):
        return lax.dynamic_slice_in_dim(w_uvqk, owner * 512, 512, 1)

    pieces = [columns(y)] + [
        lax.ppermute(columns((y + k) & 3), "y", [(i, (i + k) % 4) for i in range(4)])
        for k in range(1, 4)
    ]
    piece = jnp.stack(pieces)
    mine = jnp.stack([piece] + [lax.ppermute(piece, ("zl", "zh"), z_shift(k)) for k in range(1, 8)])
    other = lax.ppermute(mine, "core", [(0, 1), (1, 0)])

    runs = jnp.concatenate(rotations(tokens, "y", 4), axis=0)
    chunks = rotations(runs, "x", 4)

    kv, uq = call(
        project_kernel,
        [jax.ShapeDtypeStruct((4, RUN, 2 * DH), bf16)] * 2,
        1,
        6,
        [pltpu.VMEM((1024, 512), bf16), pltpu.VMEM((512, 512), jnp.float32)],
        2 * 512 * 512 * 4096,
        9 * 2**20,
        "project",
    )(place, *chunks, mine, other)

    kv_all = lax.all_gather(kv, plane)

    wo = rotations(wo_and_ids[:, :64], "y", 4)
    coded = wo_and_ids[::4, 64:72].astype(jnp.int32).reshape(4, 4, 2, TILE)
    k_ids = (coded[:, :, 0] * 128 + coded[:, :, 1]).transpose(1, 0, 2)
    q_ids = lax.dynamic_slice(k_ids, (0, zl * 2 + core, zh * RUN), (4, 1, RUN)).reshape(4, RUN, 1)
    q_edges = jnp.concatenate([q_ids[:, 0], q_ids[:, -1]], axis=1)
    k_edges = jnp.stack([k_ids[:, :, 0], k_ids[:, :, -1]], axis=-1).reshape(16, 2)
    head = x * 4 + y
    biases = lax.dynamic_slice(rab_table, (head, 0), (1, NB))
    gain = lax.dynamic_slice(norm_gain, (head, 0), (1, DH))
    table = jnp.pad(biases, ((0, 0), (0, DH - NB)))

    gated = call(
        attend_kernel,
        jax.ShapeDtypeStruct((4, RUN, DH), bf16),
        5,
        6,
        [pltpu.VMEM((RUN, DH), jnp.float32)],
        4 * 512 * 4096 * DH,
        5 * 2**20,
        "attend",
    )(place, user_lengths, q_edges, k_edges, biases[0], kv_all, uq, q_ids, k_ids, table, gain)

    own = [gated[0]] + [
        lax.ppermute(gated[k], "y", [(i, (i - k) % 4) for i in range(4)]) for k in range(1, 4)
    ]
    heads = jnp.stack(rotations(jnp.concatenate(own, axis=1), "x", 4))

    return call(
        output_kernel,
        jax.ShapeDtypeStruct((RUN, 1024), bf16),
        1,
        6,
        [pltpu.VMEM((RUN, 2048), bf16)],
        2 * RUN * 2048 * 1024,
        5 * 2**20,
        "project_out",
    )(place, tokens, heads, *wo)


def solution(mesh):
    fine = Mesh(mesh.devices.reshape(4, 2, 2, 4, 4), ("y", "zl", "core", "zh", "x"))
    every = ("y", "zl", "core", "zh")
    placed = (
        P(every, "x"),
        P(every, "x"),
        P("x", every),
        P(),
        P(),
        P(),
        P(("y", "zl", "core")),
    )
    return jax.shard_map(
        on_device, mesh=fine, in_specs=placed, out_specs=P(every, "x"), check_vma=False
    )
```

```python
import functools

import jax
import jax.numpy as jnp
from jax import lax
from jax.experimental import pallas as pl
from jax.experimental.pallas import tpu as pltpu
from jax.sharding import Mesh
from jax.sharding import PartitionSpec as P

DH = 128
NB = 32
RUN = 128
BLOCK = 512
PAIR = 256
NORM_EPS = 1e-05
SCALE = DH ** (-0.5)


def rotations(value, axis, size, step=1):
    return [value] + [
        lax.ppermute(value, axis, [(i, (i + step * k) % size) for i in range(size)])
        for k in range(1, size)
    ]


def swap(value, axis):
    return lax.ppermute(value, axis, [(0, 1), (1, 0)])


def project_kernel(place, a0, a1, a2, a3, b0, b1, b2, b3, weights, kv_ref, q_ref, u_ref, total):
    y, x = place[0], place[4]
    seconds = (b0, b1, b2, b3)
    for kx, first in enumerate((a0, a1, a2, a3)):
        ky = (y - (x - kx)) & 3
        second = jnp.concatenate([b[kx * RUN : (kx + 1) * RUN, :] for b in seconds], axis=0)
        for m in range(4):
            left = first[...] if m < 2 else second
            right = jnp.concatenate([weights[j * 4 + m, ky, :64, :] for j in range(4)], axis=0)
            part = jnp.dot(
                left[:, (m & 1) * 256 : (m & 1) * 256 + 256], right, preferred_element_type=jnp.float32
            )
            if kx == 0 and m == 0:
                total[...] = part
            else:
                total[...] += part
    half = 0.5 * total[...]
    act = (half + half * jnp.tanh(half)).astype(jnp.bfloat16)
    for r in range(4):
        rows = slice(r * RUN, (r + 1) * RUN)
        u_ref[r] = act[rows, :DH]
        kv_ref[r, :, :DH] = act[rows, DH : 2 * DH]
        q_ref[r] = act[rows, 2 * DH : 3 * DH]
        kv_ref[r, :, DH:] = act[rows, 3 * DH :]


def attend_kernel(
    place,
    lengths,
    q_edges,
    k_edges,
    biases,
    q0,
    q1,
    q2,
    q3,
    kv_near,
    kv_far,
    q_ids,
    k_ids,
    table,
    own_ref,
    send_ref,
    queries,
    acc,
):
    y, zl, core, zh = (place[i] for i in range(4))
    block = zl * 2 + core
    end0 = lengths[0]
    end1 = end0 + lengths[1]
    end2 = end1 + lengths[2]

    def user_start(pos):
        return jnp.where(
            pos >= end2, end2, jnp.where(pos >= end1, end1, jnp.where(pos >= end0, end0, 0))
        )

    for kz, source in enumerate((q0, q1, q2, q3)):
        rows = pl.ds(pl.multiple_of(((zh - kz) & 3) * RUN, RUN), RUN)
        for r in range(4):
            queries[r, rows, :] = source[r]
    table_rows = jnp.broadcast_to(table[...], (PAIR, DH))

    @pl.loop(0, 4)
    def _(r):
        group = (y - r) & 3
        first = group * 2048 + block * BLOCK
        start_low, start_high = user_start(first), user_start(first + BLOCK - 1)
        q_low, q_high = q_edges[r, 0], q_edges[r, 1]
        acc[...] = jnp.zeros_like(acc)

        def tile(t, carry):
            ky, zl_from = (y - (t >> 1)) & 3, t & 1
            zx = zl ^ zl_from
            near, far = kv_near[zx, ky], kv_far[zx, ky]
            keys = jnp.concatenate([near[:, DH:], far[:, DH:]], axis=0)
            values = jnp.concatenate([near[:, :DH], far[:, :DH]], axis=0)
            k_first = t * 1024 + zh * RUN
            k_last = k_first + BLOCK + RUN - 1
            gap_low = jnp.clip(q_low - k_edges[ky, zl_from * 2 + 1], 0, NB - 1)
            gap_high = jnp.clip(q_high - k_edges[ky, zl_from * 2], 0, NB - 1)
            plain = (k_last <= first) & (k_first >= start_high) & (gap_low == gap_high)

            def scores(part):
                rows = slice(part * PAIR, (part + 1) * PAIR)
                return rows, lax.dot_general(
                    queries[r, rows, :],
                    keys,
                    (((1,), (1,)), ((), ())),
                    preferred_element_type=jnp.float32,
                ) * (0.5 * SCALE)

            @pl.when(plain)
            def _():
                bias = 0.5 * biases[gap_low]
                for part in range(2):
                    rows, half = scores(part)
                    half = half + bias
                    weights = (half + half * jnp.tanh(half)).astype(jnp.bfloat16)
                    acc[rows, :] += jnp.dot(weights, values, preferred_element_type=jnp.float32)

            @pl.when(jnp.logical_not(plain))
            def _():
                k_row = k_ids[ky, pl.ds(zl_from, 1), :]
                column = lax.broadcasted_iota(jnp.int32, (1, PAIR), 1)
                k_pos = k_first + ((column >> 7) ^ core) * BLOCK + (column & (RUN - 1))
                for part in range(2):
                    rows, half = scores(part)
                    gaps = jnp.clip(q_ids[r, rows, :] - k_row, 0, NB - 1)
                    bias = jnp.concatenate(
                        [
                            jnp.take_along_axis(
                                table_rows,
                                gaps[:, c * DH : (c + 1) * DH],
                                axis=1,
                                mode="promise_in_bounds",
                            )
                            for c in range(PAIR // DH)
                        ],
                        axis=1,
                    )
                    half = half + 0.5 * bias
                    q_pos = first + part * PAIR + lax.broadcasted_iota(jnp.int32, (PAIR, 1), 0)
                    seen = (k_pos <= q_pos) & (k_pos >= user_start(q_pos))
                    silu = half + half * jnp.tanh(half)
                    weights = jnp.where(seen, silu, 0.0).astype(jnp.bfloat16)
                    acc[rows, :] += jnp.dot(weights, values, preferred_element_type=jnp.float32)

            return carry

        lowest = jnp.maximum((start_low - (BLOCK + RUN - 1) - zh * RUN + 1023) >> 10, 0)
        lax.fori_loop(lowest, group * 2 + zl + 1, tile, 0)
        own_ref[r] = acc[pl.ds(pl.multiple_of(zh * RUN, RUN), RUN), :]
        for k in range(1, 4):
            rows = pl.ds(pl.multiple_of(((zh + k) & 3) * RUN, RUN), RUN)
            send_ref[k - 1, r] = acc[rows, :].astype(jnp.bfloat16)


def gate_kernel(own, p1, p2, p3, u, gain, out_ref):
    attended = own[...]
    for part in (p1, p2, p3):
        attended += part[...].astype(jnp.float32)
    mean = jnp.mean(attended, axis=-1, keepdims=True)
    centered = attended - mean
    var = jnp.mean(centered * centered, axis=-1, keepdims=True)
    normed = centered * lax.rsqrt(var + NORM_EPS) * gain[...]
    out_ref[...] = (normed * u[...].astype(jnp.float32)).astype(jnp.bfloat16)


def output_kernel(place, tokens, gated, weights, out_ref, rows):
    y, x = place[0], place[4]
    for kx in range(4):
        for k in range(4):
            head = ((x - kx) & 3) * 4 + ((y + k) & 3)
            rows[:, pl.ds(pl.multiple_of(head * DH, DH), DH)] = gated[kx, :, k * DH : (k + 1) * DH]
    for m in range(4):
        columns = slice(m * 256, (m + 1) * 256)
        total = tokens[:, columns].astype(jnp.float32)
        for ky in range(4):
            source = (y - ky) & 3
            left = rows[:, pl.ds(pl.multiple_of(source * 512, 512), 512)]
            right = jnp.concatenate([weights[j * 4 + m, ky] for j in range(4)], axis=0)
            total += lax.dot_general(
                left, right, (((1,), (1,)), ((), ())), preferred_element_type=jnp.float32
            )
        out_ref[:, columns] = total.astype(jnp.bfloat16)


def call(kernel, shapes, n_smem, n_vmem, scratch, flops, moved, name):
    return pl.pallas_call(
        kernel,
        out_shape=shapes,
        in_specs=[pl.BlockSpec(memory_space=pltpu.SMEM)] * n_smem
        + [pl.BlockSpec(memory_space=pltpu.VMEM)] * n_vmem,
        out_specs=jax.tree.map(lambda _: pl.BlockSpec(memory_space=pltpu.VMEM), shapes),
        scratch_shapes=scratch,
        compiler_params=pltpu.CompilerParams(vmem_limit_bytes=40 * 2**20),
        cost_estimate=pl.CostEstimate(flops=flops, bytes_accessed=moved, transcendentals=0),
        name=name,
    )


def on_device(tokens, w_uvqk, w_out, rab_table, norm_gain, user_lengths, bucket_ids):
    bf16, f32 = jnp.bfloat16, jnp.float32
    y, zl, core, zh, x = (lax.axis_index(a) for a in ("y", "zl", "core", "zh", "x"))
    place = jnp.stack([y, zl, core, zh, x]).astype(jnp.int32)
    plane = ("zh", "zl", "core")

    ids = jnp.stack([bucket_ids // 128, bucket_ids % 128]).astype(bf16)
    ids = jnp.concatenate([ids, jnp.zeros((14, BLOCK), bf16)], axis=0)

    def columns(owner):
        part = lax.dynamic_slice_in_dim(w_uvqk, owner * 512, 512, 1)
        return jnp.concatenate([part, ids], axis=0)

    pieces = [columns(y)] + [
        lax.ppermute(columns((y + k) & 3), "y", [(i, (i + k) % 4) for i in range(4)])
        for k in range(1, 4)
    ]
    piece = jnp.stack(pieces)
    weights = lax.all_gather(piece, plane)

    first = jnp.concatenate(rotations(tokens[:, :512], "y", 4), axis=0)
    second = jnp.concatenate(rotations(tokens[:, 512:], "x", 4), axis=0)
    firsts = rotations(first, "x", 4)
    seconds = rotations(second, "y", 4)

    late, _ = lax.optimization_barrier((w_out.T, (first, second)))
    swapped = lax.ppermute(late, ("y", "x"), [(b * 4 + a, a * 4 + b) for a in range(4) for b in range(4)])
    wo = jnp.stack(rotations(swapped, "y", 4))

    kv, q, u = call(
        project_kernel,
        [
            jax.ShapeDtypeStruct((4, RUN, 2 * DH), bf16),
            jax.ShapeDtypeStruct((4, RUN, DH), bf16),
            jax.ShapeDtypeStruct((4, RUN, DH), bf16),
        ],
        1,
        9,
        [pltpu.VMEM((512, 512), f32)],
        2 * 512 * 512 * 4096,
        9 * 2**20,
        "project",
    )(place, *firsts, *seconds, weights)

    wo, _ = lax.optimization_barrier((wo, kv))
    wo_all = lax.all_gather(wo, plane)

    kv_near = jnp.stack([kv, swap(kv, "zl")])
    kv_far = swap(kv_near, "core")
    q_all = rotations(q, "zh", 4)

    coded = weights[:4, :, 64:66].astype(jnp.int32)
    all_ids = (coded[:, :, 0] * 128 + coded[:, :, 1]).transpose(1, 0, 2)
    q_ids = lax.dynamic_slice(all_ids, (0, zl * 2 + core, 0), (4, 1, BLOCK)).reshape(4, BLOCK, 1)
    k_ids = lax.dynamic_slice(all_ids, (0, 0, zh * RUN), (4, 4, RUN))
    q_edges = jnp.concatenate([q_ids[:, 0], q_ids[:, -1]], axis=1)
    k_edges = jnp.stack([k_ids[:, ::2, 0], k_ids[:, 1::2, -1]], axis=-1).reshape(4, 4)
    k_pairs = k_ids.reshape(4, 2, 2, RUN)
    k_pairs = jnp.where(core == 0, k_pairs, k_pairs[:, :, ::-1]).reshape(4, 2, PAIR)
    head = x * 4 + y
    biases = lax.dynamic_slice(rab_table, (head, 0), (1, NB))
    gain = lax.dynamic_slice(norm_gain, (head, 0), (1, DH))
    table = jnp.pad(biases, ((0, 0), (0, DH - NB)))

    own, parts = call(
        attend_kernel,
        [jax.ShapeDtypeStruct((4, RUN, DH), f32), jax.ShapeDtypeStruct((3, 4, RUN, DH), bf16)],
        5,
        9,
        [pltpu.VMEM((4, BLOCK, DH), bf16), pltpu.VMEM((BLOCK, DH), f32)],
        4 * 512 * 4096 * DH,
        5 * 2**20,
        "attend",
    )(place, user_lengths, q_edges, k_edges, biases[0], *q_all, kv_near, kv_far, q_ids, k_pairs, table)

    arrived = [
        lax.ppermute(parts[k - 1], "zh", [(i, (i + k) % 4) for i in range(4)]) for k in range(1, 4)
    ]
    gated = call(
        gate_kernel,
        jax.ShapeDtypeStruct((4, RUN, DH), bf16),
        0,
        6,
        [],
        20 * 512 * DH,
        2**20,
        "gate",
    )(own, *arrived, u, gain)

    owned = [gated[0]] + [
        lax.ppermute(gated[k], "y", [(i, (i - k) % 4) for i in range(4)]) for k in range(1, 4)
    ]
    heads = jnp.stack(rotations(jnp.concatenate(owned, axis=1), "x", 4))

    return call(
        output_kernel,
        jax.ShapeDtypeStruct((RUN, 1024), bf16),
        1,
        3,
        [pltpu.VMEM((RUN, 2048), bf16)],
        2 * RUN * 2048 * 1024,
        5 * 2**20,
        "project_out",
    )(place, tokens, heads, wo_all)


def solution(mesh):
    fine = Mesh(mesh.devices.reshape(4, 2, 2, 4, 4), ("y", "zl", "core", "zh", "x"))
    every = ("y", "zl", "core", "zh")
    placed = (
        P(every, "x"),
        P(every, "x"),
        P("x", every),
        P(),
        P(),
        P(),
        P(("y", "zl", "core")),
    )
    return jax.shard_map(
        on_device, mesh=fine, in_specs=placed, out_specs=P(every, "x"), check_vma=False
    )
```

```python
import functools

import jax
import jax.numpy as jnp
from jax import lax
from jax.experimental import pallas as pl
from jax.experimental.pallas import tpu as pltpu
from jax.sharding import Mesh
from jax.sharding import PartitionSpec as P

DH = 128
NB = 32
RUN = 128
BLOCK = 512
PAIR = 256
NORM_EPS = 1e-05
SCALE = DH ** (-0.5)


def rotations(value, axis, size, step=1):
    return [value] + [
        lax.ppermute(value, axis, [(i, (i + step * k) % size) for i in range(size)])
        for k in range(1, size)
    ]


def swap(value, axis):
    return lax.ppermute(value, axis, [(0, 1), (1, 0)])


def project_kernel(place, a0, a1, a2, a3, b0, b1, b2, b3, weights, kv_ref, q_ref, u_ref, total):
    y, x = place[0], place[4]
    seconds = (b0, b1, b2, b3)
    for kx, first in enumerate((a0, a1, a2, a3)):
        ky = (y - (x - kx)) & 3
        second = jnp.concatenate([b[kx * RUN : (kx + 1) * RUN, :] for b in seconds], axis=0)
        for m in range(4):
            left = first[...] if m < 2 else second
            right = jnp.concatenate([weights[j * 4 + m, ky] for j in range(4)], axis=0)
            part = jnp.dot(
                left[:, (m & 1) * 256 : (m & 1) * 256 + 256], right, preferred_element_type=jnp.float32
            )
            if kx == 0 and m == 0:
                total[...] = part
            else:
                total[...] += part
    half = 0.5 * total[...]
    act = (half + half * jnp.tanh(half)).astype(jnp.bfloat16)
    for r in range(4):
        rows = slice(r * RUN, (r + 1) * RUN)
        u_ref[r] = act[rows, :DH]
        kv_ref[r, :, :DH] = act[rows, DH : 2 * DH]
        q_ref[r] = act[rows, 2 * DH : 3 * DH]
        kv_ref[r, :, DH:] = act[rows, 3 * DH :]


def attend_kernel(
    place,
    lengths,
    q_edges,
    k_edges,
    biases,
    q0,
    q1,
    q2,
    q3,
    kv_near,
    kv_far,
    q_ids,
    k_ids,
    table,
    send_ref,
    queries,
    acc,
):
    y, zl, core, zh = (place[i] for i in range(4))
    block = zl * 2 + core
    end0 = lengths[0]
    end1 = end0 + lengths[1]
    end2 = end1 + lengths[2]

    def user_start(pos):
        return jnp.where(
            pos >= end2, end2, jnp.where(pos >= end1, end1, jnp.where(pos >= end0, end0, 0))
        )

    for kz, source in enumerate((q0, q1, q2, q3)):
        rows = pl.ds(pl.multiple_of(((zh - kz) & 3) * RUN, RUN), RUN)
        for r in range(4):
            queries[r, rows, :] = source[r]
    table_rows = jnp.broadcast_to(table[...], (PAIR, DH))

    @pl.loop(0, 4)
    def _(r):
        group = (y - r) & 3
        first = group * 2048 + block * BLOCK
        start_low, start_high = user_start(first), user_start(first + BLOCK - 1)
        q_low, q_high = q_edges[r, 0], q_edges[r, 1]
        acc[...] = jnp.zeros_like(acc)

        def tile(t, carry):
            ky, zl_from = (y - (t >> 1)) & 3, t & 1
            zx = zl ^ zl_from
            near, far = kv_near[zx, ky], kv_far[zx, ky]
            keys = jnp.concatenate([near[:, DH:], far[:, DH:]], axis=0)
            values = jnp.concatenate([near[:, :DH], far[:, :DH]], axis=0)
            k_first = t * 1024 + zh * RUN
            k_last = k_first + BLOCK + RUN - 1
            gap_low = jnp.clip(q_low - k_edges[ky, zx * 2 + 1], 0, NB - 1)
            gap_high = jnp.clip(q_high - k_edges[ky, zx * 2], 0, NB - 1)
            plain = (k_last <= first) & (k_first >= start_high) & (gap_low == gap_high)

            def scores(part):
                rows = slice(part * PAIR, (part + 1) * PAIR)
                return rows, lax.dot_general(
                    queries[r, rows, :],
                    keys,
                    (((1,), (1,)), ((), ())),
                    preferred_element_type=jnp.float32,
                ) * (0.5 * SCALE)

            @pl.when(plain)
            def _():
                bias = 0.5 * biases[gap_low]
                for part in range(2):
                    rows, half = scores(part)
                    half = half + bias
                    weights = (half + half * jnp.tanh(half)).astype(jnp.bfloat16)
                    acc[rows, :] += jnp.dot(weights, values, preferred_element_type=jnp.float32)

            @pl.when(jnp.logical_not(plain))
            def _():
                k_row = k_ids[ky, pl.ds(zx, 1), :]
                column = lax.broadcasted_iota(jnp.int32, (1, PAIR), 1)
                k_pos = k_first + ((column >> 7) ^ core) * BLOCK + (column & (RUN - 1))
                for part in range(2):
                    rows, half = scores(part)
                    gaps = jnp.clip(q_ids[r, rows, :] - k_row, 0, NB - 1)
                    bias = jnp.concatenate(
                        [
                            jnp.take_along_axis(
                                table_rows,
                                gaps[:, c * DH : (c + 1) * DH],
                                axis=1,
                                mode="promise_in_bounds",
                            )
                            for c in range(PAIR // DH)
                        ],
                        axis=1,
                    )
                    half = half + 0.5 * bias
                    q_pos = first + part * PAIR + lax.broadcasted_iota(jnp.int32, (PAIR, 1), 0)
                    seen = (k_pos <= q_pos) & (k_pos >= user_start(q_pos))
                    silu = half + half * jnp.tanh(half)
                    weights = jnp.where(seen, silu, 0.0).astype(jnp.bfloat16)
                    acc[rows, :] += jnp.dot(weights, values, preferred_element_type=jnp.float32)

            return carry

        lowest = jnp.maximum((start_low - (BLOCK + RUN - 1) - zh * RUN + 1023) >> 10, 0)
        lax.fori_loop(lowest, group * 2 + zl + 1, tile, 0)
        attended = acc[...]
        centered = attended - jnp.mean(attended, axis=-1, keepdims=True)
        for zh_to in range(4):
            rows = slice(zh_to * RUN, (zh_to + 1) * RUN)
            send_ref[group * 4 + zh_to] = centered[rows, :].astype(jnp.bfloat16)


def gate_kernel(place, parts, u0, u1, u2, u3, gain, out_ref):
    y = place[0]
    for k, u in enumerate((u0, u1, u2, u3)):
        head = (y + k) & 3
        attended = parts[head * 4].astype(jnp.float32)
        for part in range(1, 4):
            attended += parts[head * 4 + part].astype(jnp.float32)
        mean = jnp.mean(attended, axis=-1, keepdims=True)
        centered = attended - mean
        var = jnp.mean(centered * centered, axis=-1, keepdims=True)
        normed = centered * lax.rsqrt(var + NORM_EPS) * gain[pl.ds(head, 1), :]
        columns = pl.ds(pl.multiple_of(head * DH, DH), DH)
        out_ref[:, columns] = (normed * u[...].astype(jnp.float32)).astype(jnp.bfloat16)


def output_kernel(place, tokens, gated, near, far, out_ref):
    y, core, x = place[0], place[2], place[4]
    for zl in range(2):
        for c, source in enumerate((near, far)):
            block = zl * 2 + (core ^ c)
            columns = pl.ds(pl.multiple_of(block * 256, 256), 256)
            total = tokens[:, columns].astype(jnp.float32)
            for ky in range(4):
                left = gated[(x - (y - ky)) & 3]
                right = jnp.concatenate([source[ky, j * 2 + zl] for j in range(4)], axis=0)
                total += lax.dot_general(
                    left, right, (((1,), (1,)), ((), ())), preferred_element_type=jnp.float32
                )
            out_ref[:, columns] = total.astype(jnp.bfloat16)


def call(kernel, shapes, n_smem, n_vmem, scratch, flops, moved, vmem, name):
    return pl.pallas_call(
        kernel,
        out_shape=shapes,
        in_specs=[pl.BlockSpec(memory_space=pltpu.SMEM)] * n_smem
        + [pl.BlockSpec(memory_space=pltpu.VMEM)] * n_vmem,
        out_specs=jax.tree.map(lambda _: pl.BlockSpec(memory_space=pltpu.VMEM), shapes),
        scratch_shapes=scratch,
        compiler_params=pltpu.CompilerParams(vmem_limit_bytes=vmem * 2**20),
        cost_estimate=pl.CostEstimate(flops=flops, bytes_accessed=moved, transcendentals=0),
        name=name,
    )


def on_device(tokens, w_uvqk, w_out, rab_table, norm_gain, user_lengths, bucket_ids):
    bf16, f32 = jnp.bfloat16, jnp.float32
    y, zl, core, zh, x = (lax.axis_index(a) for a in ("y", "zl", "core", "zh", "x"))
    place = jnp.stack([y, zl, core, zh, x]).astype(jnp.int32)
    plane = ("zh", "zl", "core")

    def columns(owner):
        return lax.dynamic_slice_in_dim(w_uvqk, owner * 512, 512, 1)

    pieces = [columns(y)] + [
        lax.ppermute(columns((y + k) & 3), "y", [(i, (i + k) % 4) for i in range(4)])
        for k in range(1, 4)
    ]
    piece = jnp.stack(pieces)
    weights = lax.all_gather(piece, plane)

    first = rotations(tokens[:, :512], "y", 4)
    second = rotations(tokens[:, 512:], "x", 4)
    first, second = lax.optimization_barrier((first, second))
    firsts = rotations(jnp.concatenate(first, axis=0), "x", 4)
    seconds = rotations(jnp.concatenate(second, axis=0), "y", 4)

    ids, late, _ = lax.optimization_barrier((bucket_ids, w_out.T, (first, second)))
    ids_y = jnp.stack(rotations(ids, "y", 4))
    ids_near = jnp.stack([ids_y, swap(ids_y, "zl")])
    ids_far = swap(ids_near, "core")
    swapped = lax.ppermute(late, ("y", "x"), [(b * 4 + a, a * 4 + b) for a in range(4) for b in range(4)])

    firsts, seconds, ids_y, ids_near, ids_far, swapped = lax.optimization_barrier(
        (firsts, seconds, ids_y, ids_near, ids_far, swapped)
    )
    kv, q, u = call(
        project_kernel,
        [
            jax.ShapeDtypeStruct((4, RUN, 2 * DH), bf16),
            jax.ShapeDtypeStruct((4, RUN, DH), bf16),
            jax.ShapeDtypeStruct((4, RUN, DH), bf16),
        ],
        1,
        9,
        [pltpu.VMEM((512, 512), f32)],
        2 * 512 * 512 * 4096,
        9 * 2**20,
        24,
        "project",
    )(place, *firsts, *seconds, weights)

    wo_block = lax.all_gather(swapped, plane)

    kv_near = jnp.stack([kv, swap(kv, "zl")])
    kv_far = swap(kv_near, "core")
    q, _ = lax.optimization_barrier((q, kv_near))
    q_all = rotations(q, "zh", 4)

    q_ids = ids_y.reshape(4, BLOCK, 1)
    k_ids = lax.dynamic_slice(jnp.stack([ids_near, ids_far]), (0, 0, 0, zh * RUN), (2, 2, 4, RUN))
    k_edges = jnp.stack([jnp.min(k_ids[..., 0], axis=0), jnp.max(k_ids[..., -1], axis=0)], axis=-1)
    k_edges = k_edges.transpose(1, 0, 2).reshape(4, 4)
    k_ids = k_ids.transpose(2, 1, 0, 3).reshape(4, 2, PAIR)
    q_edges = jnp.stack([ids_y[:, 0], ids_y[:, -1]], axis=1)
    biases = lax.dynamic_slice(rab_table, (x * 4 + y, 0), (1, NB))
    gains = lax.dynamic_slice(norm_gain, (x * 4, 0), (4, DH))
    table = jnp.pad(biases, ((0, 0), (0, DH - NB)))

    parts = call(
        attend_kernel,
        jax.ShapeDtypeStruct((16, RUN, DH), bf16),
        5,
        9,
        [pltpu.VMEM((4, BLOCK, DH), bf16), pltpu.VMEM((BLOCK, DH), f32)],
        4 * 512 * 4096 * DH,
        5 * 2**20,
        14,
        "attend",
    )(place, user_lengths, q_edges, k_edges, biases[0], *q_all, kv_near, kv_far, q_ids, k_ids, table)

    half = lax.dynamic_index_in_dim(wo_block.reshape(8, 2, 64, 512), core, 1, keepdims=False)
    half, u, _ = lax.optimization_barrier((half, u, (kv_far, q_all)))
    u_own = [u[0]] + [
        lax.ppermute(u[k], "y", [(i, (i - k) % 4) for i in range(4)]) for k in range(1, 4)
    ]
    wo_parts = rotations(half, "y", 4)

    arrived = lax.all_to_all(parts, ("y", "zh"), 0, 0, tiled=True)
    gated = call(
        gate_kernel,
        jax.ShapeDtypeStruct((RUN, 4 * DH), bf16),
        1,
        6,
        [],
        20 * 512 * DH,
        2**20,
        4,
        "gate",
    )(place, arrived, *u_own, gains)
    wo_parts, gated = lax.optimization_barrier((wo_parts, gated))
    heads = jnp.stack(rotations(gated, "x", 4))
    wo_near = jnp.stack(wo_parts)
    wo_far = swap(wo_near, "core")

    return call(
        output_kernel,
        jax.ShapeDtypeStruct((RUN, 1024), bf16),
        1,
        4,
        [],
        2 * RUN * 2048 * 1024,
        5 * 2**20,
        14,
        "project_out",
    )(place, tokens, heads, wo_near, wo_far)


def solution(mesh):
    fine = Mesh(mesh.devices.reshape(4, 2, 2, 4, 4), ("y", "zl", "core", "zh", "x"))
    every = ("y", "zl", "core", "zh")
    placed = (
        P(every, "x"),
        P(every, "x"),
        P("x", every),
        P(),
        P(),
        P(),
        P(("y", "zl", "core")),
    )
    return jax.shard_map(
        on_device, mesh=fine, in_specs=placed, out_specs=P(every, "x"), check_vma=False
    )
```

```python
import functools

import jax
import jax.numpy as jnp
from jax import lax
from jax.experimental import pallas as pl
from jax.experimental.pallas import tpu as pltpu
from jax.sharding import Mesh
from jax.sharding import PartitionSpec as P

DH = 128
NB = 32
RUN = 128
BLOCK = 512
PAIR = 256
NORM_EPS = 1e-05
SCALE = DH ** (-0.5)


def rotations(value, axis, size, step=1):
    return [value] + [
        lax.ppermute(value, axis, [(i, (i + step * k) % size) for i in range(size)])
        for k in range(1, size)
    ]


def swap(value, axis):
    return lax.ppermute(value, axis, [(0, 1), (1, 0)])


def project_kernel(place, a0, a1, a2, a3, b0, b1, b2, b3, weights, kv_ref, q_ref, u_ref, total):
    y, x = place[0], place[4]
    seconds = (b0, b1, b2, b3)
    for kx, first in enumerate((a0, a1, a2, a3)):
        ky = (y - (x - kx)) & 3
        second = jnp.concatenate([b[kx * RUN : (kx + 1) * RUN, :] for b in seconds], axis=0)
        for m in range(4):
            left = first[...] if m < 2 else second
            right = jnp.concatenate([weights[j * 4 + m, ky] for j in range(4)], axis=0)
            part = jnp.dot(
                left[:, (m & 1) * 256 : (m & 1) * 256 + 256], right, preferred_element_type=jnp.float32
            )
            if kx == 0 and m == 0:
                total[...] = part
            else:
                total[...] += part
    half = 0.5 * total[...]
    act = (half + half * jnp.tanh(half)).astype(jnp.bfloat16)
    for r in range(4):
        rows = slice(r * RUN, (r + 1) * RUN)
        u_ref[r] = act[rows, :DH]
        kv_ref[r, :, :DH] = act[rows, DH : 2 * DH]
        q_ref[r] = act[rows, 2 * DH : 3 * DH]
        kv_ref[r, :, DH:] = act[rows, 3 * DH :]


def attend_kernel(
    place,
    lengths,
    q_edges,
    k_edges,
    biases,
    q0,
    q1,
    q2,
    q3,
    kv_near,
    kv_far,
    q_ids,
    k_ids,
    table,
    send_ref,
    queries,
    acc,
):
    y, zl, core, zh = (place[i] for i in range(4))
    block = zl * 2 + core
    end0 = lengths[0]
    end1 = end0 + lengths[1]
    end2 = end1 + lengths[2]

    def user_start(pos):
        return jnp.where(
            pos >= end2, end2, jnp.where(pos >= end1, end1, jnp.where(pos >= end0, end0, 0))
        )

    for kz, source in enumerate((q0, q1, q2, q3)):
        rows = pl.ds(pl.multiple_of(((zh - kz) & 3) * RUN, RUN), RUN)
        for r in range(4):
            queries[r, rows, :] = source[r]
    table_rows = jnp.broadcast_to(table[...], (PAIR, DH))

    @pl.loop(0, 4)
    def _(r):
        group = (y - r) & 3
        first = group * 2048 + block * BLOCK
        start_low, start_high = user_start(first), user_start(first + BLOCK - 1)
        q_low, q_high = q_edges[r, 0], q_edges[r, 1]
        acc[...] = jnp.zeros_like(acc)

        def tile(t, carry):
            ky, zl_from = (y - (t >> 1)) & 3, t & 1
            zx = zl ^ zl_from
            near, far = kv_near[zx, ky], kv_far[zx, ky]
            keys = jnp.concatenate([near[:, DH:], far[:, DH:]], axis=0)
            values = jnp.concatenate([near[:, :DH], far[:, :DH]], axis=0)
            k_first = t * 1024 + zh * RUN
            k_last = k_first + BLOCK + RUN - 1
            gap_low = jnp.clip(q_low - k_edges[ky, zx * 2 + 1], 0, NB - 1)
            gap_high = jnp.clip(q_high - k_edges[ky, zx * 2], 0, NB - 1)
            plain = (k_last <= first) & (k_first >= start_high) & (gap_low == gap_high)

            def scores(part):
                rows = slice(part * PAIR, (part + 1) * PAIR)
                return rows, lax.dot_general(
                    queries[r, rows, :],
                    keys,
                    (((1,), (1,)), ((), ())),
                    preferred_element_type=jnp.float32,
                ) * (0.5 * SCALE)

            @pl.when(plain)
            def _():
                bias = 0.5 * biases[gap_low]
                for part in range(2):
                    rows, half = scores(part)
                    half = half + bias
                    weights = (half + half * jnp.tanh(half)).astype(jnp.bfloat16)
                    acc[rows, :] += jnp.dot(weights, values, preferred_element_type=jnp.float32)

            @pl.when(jnp.logical_not(plain))
            def _():
                k_row = k_ids[ky, pl.ds(zx, 1), :]
                column = lax.broadcasted_iota(jnp.int32, (1, PAIR), 1)
                k_pos = k_first + ((column >> 7) ^ core) * BLOCK + (column & (RUN - 1))
                for part in range(2):
                    rows, half = scores(part)
                    gaps = jnp.clip(q_ids[r, rows, :] - k_row, 0, NB - 1)
                    bias = jnp.concatenate(
                        [
                            jnp.take_along_axis(
                                table_rows,
                                gaps[:, c * DH : (c + 1) * DH],
                                axis=1,
                                mode="promise_in_bounds",
                            )
                            for c in range(PAIR // DH)
                        ],
                        axis=1,
                    )
                    half = half + 0.5 * bias
                    q_pos = first + part * PAIR + lax.broadcasted_iota(jnp.int32, (PAIR, 1), 0)
                    seen = (k_pos <= q_pos) & (k_pos >= user_start(q_pos))
                    silu = half + half * jnp.tanh(half)
                    weights = jnp.where(seen, silu, 0.0).astype(jnp.bfloat16)
                    acc[rows, :] += jnp.dot(weights, values, preferred_element_type=jnp.float32)

            return carry

        lowest = jnp.maximum((start_low - (BLOCK + RUN - 1) - zh * RUN + 1023) >> 10, 0)
        lax.fori_loop(lowest, group * 2 + zl + 1, tile, 0)
        attended = acc[...]
        centered = attended - jnp.mean(attended, axis=-1, keepdims=True)
        for zh_to in range(4):
            rows = slice(zh_to * RUN, (zh_to + 1) * RUN)
            send_ref[group * 4 + zh_to] = centered[rows, :].astype(jnp.bfloat16)


def gate_kernel(place, parts, u0, u1, u2, u3, gain, out_ref):
    y = place[0]
    for k, u in enumerate((u0, u1, u2, u3)):
        head = (y + k) & 3
        attended = parts[head * 4].astype(jnp.float32)
        for part in range(1, 4):
            attended += parts[head * 4 + part].astype(jnp.float32)
        mean = jnp.mean(attended, axis=-1, keepdims=True)
        centered = attended - mean
        var = jnp.mean(centered * centered, axis=-1, keepdims=True)
        normed = centered * lax.rsqrt(var + NORM_EPS) * gain[pl.ds(head, 1), :]
        columns = pl.ds(pl.multiple_of(head * DH, DH), DH)
        out_ref[:, columns] = (normed * u[...].astype(jnp.float32)).astype(jnp.bfloat16)


def output_kernel(place, tokens, gated, weights, out_ref):
    y, x = place[0], place[4]
    for m in range(4):
        columns = slice(m * 256, (m + 1) * 256)
        total = tokens[:, columns].astype(jnp.float32)
        for ky in range(4):
            left = gated[(x - (y - ky)) & 3]
            right = jnp.concatenate([weights[j * 4 + m, ky] for j in range(4)], axis=0)
            total += lax.dot_general(
                left, right, (((1,), (1,)), ((), ())), preferred_element_type=jnp.float32
            )
        out_ref[:, columns] = total.astype(jnp.bfloat16)


def call(kernel, shapes, n_smem, n_vmem, scratch, flops, moved, vmem, name):
    return pl.pallas_call(
        kernel,
        out_shape=shapes,
        in_specs=[pl.BlockSpec(memory_space=pltpu.SMEM)] * n_smem
        + [pl.BlockSpec(memory_space=pltpu.VMEM)] * n_vmem,
        out_specs=jax.tree.map(lambda _: pl.BlockSpec(memory_space=pltpu.VMEM), shapes),
        scratch_shapes=scratch,
        compiler_params=pltpu.CompilerParams(vmem_limit_bytes=vmem * 2**20),
        cost_estimate=pl.CostEstimate(flops=flops, bytes_accessed=moved, transcendentals=0),
        name=name,
    )


def on_device(tokens, w_uvqk, w_out, rab_table, norm_gain, user_lengths, bucket_ids):
    bf16, f32 = jnp.bfloat16, jnp.float32
    y, zl, core, zh, x = (lax.axis_index(a) for a in ("y", "zl", "core", "zh", "x"))
    place = jnp.stack([y, zl, core, zh, x]).astype(jnp.int32)
    plane = ("zh", "zl", "core")

    def columns(owner):
        return lax.dynamic_slice_in_dim(w_uvqk, owner * 512, 512, 1)

    pieces = [columns(y)] + [
        lax.ppermute(columns((y + k) & 3), "y", [(i, (i + k) % 4) for i in range(4)])
        for k in range(1, 4)
    ]
    piece = jnp.stack(pieces)
    weights = lax.all_gather(piece, plane)

    first = rotations(tokens[:, :512], "y", 4)
    second = rotations(tokens[:, 512:], "x", 4)
    first, second = lax.optimization_barrier((first, second))
    firsts = rotations(jnp.concatenate(first, axis=0), "x", 4)
    seconds = rotations(jnp.concatenate(second, axis=0), "y", 4)

    ids, late, _ = lax.optimization_barrier((bucket_ids, w_out.T, (firsts[1:3], seconds[1:3])))
    ids_y = jnp.stack(rotations(ids, "y", 4))
    ids_near = jnp.stack([ids_y, swap(ids_y, "zl")])
    ids_far = swap(ids_near, "core")
    swapped = lax.ppermute(late, ("y", "x"), [(b * 4 + a, a * 4 + b) for a in range(4) for b in range(4)])
    wo_rows = jnp.stack(rotations(swapped, "y", 4))

    firsts, seconds, ids_y, ids_near, ids_far, wo_rows = lax.optimization_barrier(
        (firsts, seconds, ids_y, ids_near, ids_far, wo_rows)
    )
    kv, q, u = call(
        project_kernel,
        [
            jax.ShapeDtypeStruct((4, RUN, 2 * DH), bf16),
            jax.ShapeDtypeStruct((4, RUN, DH), bf16),
            jax.ShapeDtypeStruct((4, RUN, DH), bf16),
        ],
        1,
        9,
        [pltpu.VMEM((512, 512), f32)],
        2 * 512 * 512 * 4096,
        9 * 2**20,
        24,
        "project",
    )(place, *firsts, *seconds, weights)

    wo_rows, _ = lax.optimization_barrier((wo_rows, kv))
    wo_all = lax.all_gather(wo_rows, plane)

    kv_near = jnp.stack([kv, swap(kv, "zl")])
    kv_far = swap(kv_near, "core")
    q_all = rotations(q, "zh", 4)

    q_ids = ids_y.reshape(4, BLOCK, 1)
    k_ids = lax.dynamic_slice(jnp.stack([ids_near, ids_far]), (0, 0, 0, zh * RUN), (2, 2, 4, RUN))
    k_edges = jnp.stack([jnp.min(k_ids[..., 0], axis=0), jnp.max(k_ids[..., -1], axis=0)], axis=-1)
    k_edges = k_edges.transpose(1, 0, 2).reshape(4, 4)
    k_ids = k_ids.transpose(2, 1, 0, 3).reshape(4, 2, PAIR)
    q_edges = jnp.stack([ids_y[:, 0], ids_y[:, -1]], axis=1)
    biases = lax.dynamic_slice(rab_table, (x * 4 + y, 0), (1, NB))
    gains = lax.dynamic_slice(norm_gain, (x * 4, 0), (4, DH))
    table = jnp.pad(biases, ((0, 0), (0, DH - NB)))

    parts = call(
        attend_kernel,
        jax.ShapeDtypeStruct((16, RUN, DH), bf16),
        5,
        9,
        [pltpu.VMEM((4, BLOCK, DH), bf16), pltpu.VMEM((BLOCK, DH), f32)],
        4 * 512 * 4096 * DH,
        5 * 2**20,
        14,
        "attend",
    )(place, user_lengths, q_edges, k_edges, biases[0], *q_all, kv_near, kv_far, q_ids, k_ids, table)

    u, _ = lax.optimization_barrier((u, (kv_far, q_all)))
    u_own = [u[0]] + [
        lax.ppermute(u[k], "y", [(i, (i - k) % 4) for i in range(4)]) for k in range(1, 4)
    ]
    arrived = lax.all_to_all(parts, ("y", "zh"), 0, 0, tiled=True)
    gated = call(
        gate_kernel,
        jax.ShapeDtypeStruct((RUN, 4 * DH), bf16),
        1,
        6,
        [],
        20 * 512 * DH,
        2**20,
        4,
        "gate",
    )(place, arrived, *u_own, gains)
    heads = jnp.stack(rotations(gated, "x", 4))

    return call(
        output_kernel,
        jax.ShapeDtypeStruct((RUN, 1024), bf16),
        1,
        3,
        [],
        2 * RUN * 2048 * 1024,
        5 * 2**20,
        14,
        "project_out",
    )(place, tokens, heads, wo_all)


def solution(mesh):
    fine = Mesh(mesh.devices.reshape(4, 2, 2, 4, 4), ("y", "zl", "core", "zh", "x"))
    every = ("y", "zl", "core", "zh")
    placed = (
        P(every, "x"),
        P(every, "x"),
        P("x", every),
        P(),
        P(),
        P(),
        P(("y", "zl", "core")),
    )
    return jax.shard_map(
        on_device, mesh=fine, in_specs=placed, out_specs=P(every, "x"), check_vma=False
    )
```

```python
import functools

import jax
import jax.numpy as jnp
from jax import lax
from jax.experimental import pallas as pl
from jax.experimental.pallas import tpu as pltpu
from jax.sharding import Mesh
from jax.sharding import PartitionSpec as P

DH = 128
NB = 32
RUN = 128
BLOCK = 512
PAIR = 256
NORM_EPS = 1e-05
SCALE = DH ** (-0.5)


def rotations(value, axis, size, step=1):
    return [value] + [
        lax.ppermute(value, axis, [(i, (i + step * k) % size) for i in range(size)])
        for k in range(1, size)
    ]


def swap(value, axis):
    return lax.ppermute(value, axis, [(0, 1), (1, 0)])


def project_kernel(place, a0, a1, a2, a3, b0, b1, b2, b3, weights, k_rows, kv_ref, q_ref, u_ref, total):
    y, x = place[0], place[4]
    seconds = (b0, b1, b2, b3)
    for kx, first in enumerate((a0, a1, a2, a3)):
        ky = (y - (x - kx)) & 3
        second = jnp.concatenate([b[kx * RUN : (kx + 1) * RUN, :] for b in seconds], axis=0)
        for m in range(4):
            left = first[...] if m < 2 else second
            right = jnp.concatenate([weights[j * 4 + m, ky] for j in range(4)], axis=0)
            part = jnp.dot(
                left[:, (m & 1) * 256 : (m & 1) * 256 + 256], right, preferred_element_type=jnp.float32
            )
            if kx == 0 and m == 0:
                total[...] = part
            else:
                total[...] += part
    half = 0.5 * total[...]
    act = (half + half * jnp.tanh(half)).astype(jnp.bfloat16)
    for r in range(4):
        rows = slice(r * RUN, (r + 1) * RUN)
        u_ref[r] = act[rows, :DH]
        kv_ref[r, :RUN, :DH] = act[rows, DH : 2 * DH]
        q_ref[r] = act[rows, 2 * DH : 3 * DH]
        kv_ref[r, :RUN, DH:] = act[rows, 3 * DH :]
        kv_ref[r, RUN:, :] = k_rows[r]


def attend_kernel(
    place,
    lengths,
    q_edges,
    k_edges,
    biases,
    q0,
    q1,
    q2,
    q3,
    kv_near,
    kv_far,
    q_ids,
    k_ids,
    table,
    send_ref,
    queries,
    acc,
):
    y, zl, core, zh = (place[i] for i in range(4))
    block = zl * 2 + core
    end0 = lengths[0]
    end1 = end0 + lengths[1]
    end2 = end1 + lengths[2]

    def user_start(pos):
        return jnp.where(
            pos >= end2, end2, jnp.where(pos >= end1, end1, jnp.where(pos >= end0, end0, 0))
        )

    for kz, source in enumerate((q0, q1, q2, q3)):
        rows = pl.ds(pl.multiple_of(((zh - kz) & 3) * RUN, RUN), RUN)
        for r in range(4):
            queries[r, rows, :] = source[r]
    table_rows = jnp.broadcast_to(table[...], (PAIR, DH))

    @pl.loop(0, 4)
    def _(r):
        group = (y - r) & 3
        first = group * 2048 + block * BLOCK
        start_low, start_high = user_start(first), user_start(first + BLOCK - 1)
        q_low, q_high = q_edges[r, 0], q_edges[r, 1]
        acc[...] = jnp.zeros_like(acc)

        def tile(t, carry):
            ky, zl_from = (y - (t >> 1)) & 3, t & 1
            zx = zl ^ zl_from
            near, far = kv_near[zx, ky, :RUN, :], kv_far[zx, ky, :RUN, :]
            keys = jnp.concatenate([near[:, DH:], far[:, DH:]], axis=0)
            values = jnp.concatenate([near[:, :DH], far[:, :DH]], axis=0)
            k_first = t * 1024 + zh * RUN
            k_last = k_first + BLOCK + RUN - 1
            gap_low = jnp.clip(q_low - k_edges[ky, zx * 2 + 1], 0, NB - 1)
            gap_high = jnp.clip(q_high - k_edges[ky, zx * 2], 0, NB - 1)
            plain = (k_last <= first) & (k_first >= start_high) & (gap_low == gap_high)

            def scores(part):
                rows = slice(part * PAIR, (part + 1) * PAIR)
                return rows, lax.dot_general(
                    queries[r, rows, :],
                    keys,
                    (((1,), (1,)), ((), ())),
                    preferred_element_type=jnp.float32,
                ) * (0.5 * SCALE)

            @pl.when(plain)
            def _():
                bias = 0.5 * biases[gap_low]
                for part in range(2):
                    rows, half = scores(part)
                    half = half + bias
                    weights = (half + half * jnp.tanh(half)).astype(jnp.bfloat16)
                    acc[rows, :] += jnp.dot(weights, values, preferred_element_type=jnp.float32)

            @pl.when(jnp.logical_not(plain))
            def _():
                k_row = k_ids[ky, pl.ds(zx, 1), :]
                column = lax.broadcasted_iota(jnp.int32, (1, PAIR), 1)
                k_pos = k_first + ((column >> 7) ^ core) * BLOCK + (column & (RUN - 1))
                for part in range(2):
                    rows, half = scores(part)
                    gaps = jnp.clip(q_ids[r, rows, :] - k_row, 0, NB - 1)
                    bias = jnp.concatenate(
                        [
                            jnp.take_along_axis(
                                table_rows,
                                gaps[:, c * DH : (c + 1) * DH],
                                axis=1,
                                mode="promise_in_bounds",
                            )
                            for c in range(PAIR // DH)
                        ],
                        axis=1,
                    )
                    half = half + 0.5 * bias
                    q_pos = first + part * PAIR + lax.broadcasted_iota(jnp.int32, (PAIR, 1), 0)
                    seen = (k_pos <= q_pos) & (k_pos >= user_start(q_pos))
                    silu = half + half * jnp.tanh(half)
                    weights = jnp.where(seen, silu, 0.0).astype(jnp.bfloat16)
                    acc[rows, :] += jnp.dot(weights, values, preferred_element_type=jnp.float32)

            return carry

        lowest = jnp.maximum((start_low - (BLOCK + RUN - 1) - zh * RUN + 1023) >> 10, 0)
        lax.fori_loop(lowest, group * 2 + zl + 1, tile, 0)
        attended = acc[...]
        centered = attended - jnp.mean(attended, axis=-1, keepdims=True)
        for zh_to in range(4):
            rows = slice(zh_to * RUN, (zh_to + 1) * RUN)
            send_ref[group * 4 + zh_to] = centered[rows, :].astype(jnp.bfloat16)


def gate_kernel(place, parts, u0, u1, u2, u3, gain, out_ref):
    y = place[0]
    for k, u in enumerate((u0, u1, u2, u3)):
        head = (y + k) & 3
        attended = parts[head * 4].astype(jnp.float32)
        for part in range(1, 4):
            attended += parts[head * 4 + part].astype(jnp.float32)
        mean = jnp.mean(attended, axis=-1, keepdims=True)
        centered = attended - mean
        var = jnp.mean(centered * centered, axis=-1, keepdims=True)
        normed = centered * lax.rsqrt(var + NORM_EPS) * gain[pl.ds(head, 1), :]
        columns = pl.ds(pl.multiple_of(head * DH, DH), DH)
        out_ref[:, columns] = (normed * u[...].astype(jnp.float32)).astype(jnp.bfloat16)


def output_kernel(place, tokens, gated, near, far, out_ref):
    y, zl, core, zh, x = (place[i] for i in range(5))
    for zx in range(2):
        for c, source in enumerate((near, far)):
            block = (zl ^ zx) * 2 + (core ^ c)
            columns = pl.ds(pl.multiple_of(block * 256, 256), 256)
            total = tokens[:, columns].astype(jnp.float32)
            for ky in range(4):
                left = gated[(x - (y - ky)) & 3]
                right = jnp.concatenate([source[ky, zx, (zh - t) & 3] for t in range(4)], axis=0)
                total += lax.dot_general(
                    left, right, (((1,), (1,)), ((), ())), preferred_element_type=jnp.float32
                )
            out_ref[:, columns] = total.astype(jnp.bfloat16)


def call(kernel, shapes, n_smem, n_vmem, scratch, flops, moved, vmem, name):
    return pl.pallas_call(
        kernel,
        out_shape=shapes,
        in_specs=[pl.BlockSpec(memory_space=pltpu.SMEM)] * n_smem
        + [pl.BlockSpec(memory_space=pltpu.VMEM)] * n_vmem,
        out_specs=jax.tree.map(lambda _: pl.BlockSpec(memory_space=pltpu.VMEM), shapes),
        scratch_shapes=scratch,
        compiler_params=pltpu.CompilerParams(vmem_limit_bytes=vmem * 2**20),
        cost_estimate=pl.CostEstimate(flops=flops, bytes_accessed=moved, transcendentals=0),
        name=name,
    )


def on_device(tokens, w_uvqk, w_out, rab_table, norm_gain, user_lengths, bucket_ids):
    bf16, f32 = jnp.bfloat16, jnp.float32
    y, zl, core, zh, x = (lax.axis_index(a) for a in ("y", "zl", "core", "zh", "x"))
    place = jnp.stack([y, zl, core, zh, x]).astype(jnp.int32)
    plane = ("zh", "zl", "core")

    def columns(owner):
        return lax.dynamic_slice_in_dim(w_uvqk, owner * 512, 512, 1)

    pieces = [columns(y)] + [
        lax.ppermute(columns((y + k) & 3), "y", [(i, (i + k) % 4) for i in range(4)])
        for k in range(1, 4)
    ]
    piece = jnp.stack(pieces)
    weights = lax.all_gather(piece, plane)

    ids = jnp.stack([bucket_ids // 128, bucket_ids % 128]).astype(bf16)
    ids = jnp.concatenate([ids, jnp.zeros((14, BLOCK), bf16)], axis=0)
    first = rotations(jnp.concatenate([tokens[:, :512], ids], axis=0), "y", 4)
    second = rotations(tokens[:, 512:], "x", 4)
    first, second = lax.optimization_barrier((first, second))
    firsts = rotations(jnp.concatenate([f[:RUN] for f in first], axis=0), "x", 4)
    seconds = rotations(jnp.concatenate(second, axis=0), "y", 4)
    id_rows = jnp.stack([f[RUN : RUN + 2] for f in first])
    q_ids = (id_rows[:, 0].astype(f32) * 128 + id_rows[:, 1].astype(f32)).astype(jnp.int32)
    q_edges = jnp.stack([q_ids[:, 0], q_ids[:, -1]], axis=1)
    q_ids = q_ids.reshape(4, BLOCK, 1)
    k_rows = lax.dynamic_slice(id_rows, (0, 0, zh * RUN), (4, 2, RUN)).reshape(4, 1, PAIR)
    k_rows = jnp.pad(k_rows, ((0, 0), (0, 15), (0, 0)))

    late, _ = lax.optimization_barrier((w_out.T, piece))
    swapped = lax.ppermute(late, ("y", "x"), [(b * 4 + a, a * 4 + b) for a in range(4) for b in range(4)])
    over_zh = rotations(swapped, "zh", 4)
    wo_zh = jnp.stack(over_zh)
    wo_zh, _ = lax.optimization_barrier((wo_zh, (firsts[1:3], seconds[1:3])))
    wo_half = jnp.stack([wo_zh, swap(wo_zh, "zl")])
    wo_parts = rotations(wo_half, "y", 4)

    firsts, seconds, k_rows, q_ids, q_edges = lax.optimization_barrier(
        (firsts, seconds, k_rows, q_ids, q_edges)
    )
    kv, q, u = call(
        project_kernel,
        [
            jax.ShapeDtypeStruct((4, RUN + 16, 2 * DH), bf16),
            jax.ShapeDtypeStruct((4, RUN, DH), bf16),
            jax.ShapeDtypeStruct((4, RUN, DH), bf16),
        ],
        1,
        10,
        [pltpu.VMEM((512, 512), f32)],
        2 * 512 * 512 * 4096,
        9 * 2**20,
        20,
        "project",
    )(place, *firsts, *seconds, weights, k_rows)

    kv_near = jnp.stack([kv, swap(kv, "zl")])
    kv_far = swap(kv_near, "core")
    q_all = rotations(q, "zh", 4)

    k_ids = jnp.stack([kv_near[:, :, RUN], kv_far[:, :, RUN]]).astype(f32)
    k_ids = (k_ids[..., :DH] * 128 + k_ids[..., DH:]).astype(jnp.int32)
    k_edges = jnp.stack([jnp.min(k_ids[..., 0], axis=0), jnp.max(k_ids[..., -1], axis=0)], axis=-1)
    k_edges = k_edges.transpose(1, 0, 2).reshape(4, 4)
    k_ids = k_ids.transpose(2, 1, 0, 3).reshape(4, 2, PAIR)
    biases = lax.dynamic_slice(rab_table, (x * 4 + y, 0), (1, NB))
    gains = lax.dynamic_slice(norm_gain, (x * 4, 0), (4, DH))
    table = jnp.pad(biases, ((0, 0), (0, DH - NB)))
    wo_parts, q_all = lax.optimization_barrier((wo_parts, q_all))

    parts = call(
        attend_kernel,
        jax.ShapeDtypeStruct((16, RUN, DH), bf16),
        5,
        9,
        [pltpu.VMEM((4, BLOCK, DH), bf16), pltpu.VMEM((BLOCK, DH), f32)],
        4 * 512 * 4096 * DH,
        5 * 2**20,
        14,
        "attend",
    )(place, user_lengths, q_edges, k_edges, biases[0], *q_all, kv_near, kv_far, q_ids, k_ids, table)

    wo_near = jnp.stack(wo_parts)
    wo_far = swap(wo_near, "core")
    u, _ = lax.optimization_barrier((u, (kv_far, q_all)))
    u_own = [u[0]] + [
        lax.ppermute(u[k], "y", [(i, (i - k) % 4) for i in range(4)]) for k in range(1, 4)
    ]
    arrived = lax.all_to_all(parts, ("y", "zh"), 0, 0, tiled=True)
    arrived, wo_near, wo_far = lax.optimization_barrier((arrived, wo_near, wo_far))
    gated = call(
        gate_kernel,
        jax.ShapeDtypeStruct((RUN, 4 * DH), bf16),
        1,
        6,
        [],
        20 * 512 * DH,
        2**20,
        4,
        "gate",
    )(place, arrived, *u_own, gains)
    heads = jnp.stack(rotations(gated, "x", 4))

    return call(
        output_kernel,
        jax.ShapeDtypeStruct((RUN, 1024), bf16),
        1,
        4,
        [],
        2 * RUN * 2048 * 1024,
        5 * 2**20,
        14,
        "project_out",
    )(place, tokens, heads, wo_near, wo_far)


def solution(mesh):
    fine = Mesh(mesh.devices.reshape(4, 2, 2, 4, 4), ("y", "zl", "core", "zh", "x"))
    every = ("y", "zl", "core", "zh")
    placed = (
        P(every, "x"),
        P(every, "x"),
        P("x", every),
        P(),
        P(),
        P(),
        P(("y", "zl", "core")),
    )
    return jax.shard_map(
        on_device, mesh=fine, in_specs=placed, out_specs=P(every, "x"), check_vma=False
    )
```

```python
import functools

import jax
import jax.numpy as jnp
from jax import lax
from jax.experimental import pallas as pl
from jax.experimental.pallas import tpu as pltpu
from jax.sharding import Mesh
from jax.sharding import PartitionSpec as P

DH = 128
NB = 32
RUN = 128
BLOCK = 512
PAIR = 256
NORM_EPS = 1e-05
SCALE = DH ** (-0.5)


def rotations(value, axis, size, step=1):
    return [value] + [
        lax.ppermute(value, axis, [(i, (i + step * k) % size) for i in range(size)])
        for k in range(1, size)
    ]


def swap(value, axis):
    return lax.ppermute(value, axis, [(0, 1), (1, 0)])


def project_kernel(place, a0, a1, a2, a3, b0, b1, b2, b3, weights, kv_ref, q_ref, u_ref, total):
    step = pl.program_id(0)
    seconds = (b0, b1, b2, b3)
    for kx, first in enumerate((a0, a1, a2, a3)):

        @pl.when(step == kx)
        def _():
            second = jnp.concatenate([b[kx * RUN : (kx + 1) * RUN, :] for b in seconds], axis=0)
            for m in range(4):
                left = first[...] if m < 2 else second
                right = jnp.concatenate([weights[j * 4 + m, 0, :64, :] for j in range(4)], axis=0)
                part = jnp.dot(
                    left[:, (m & 1) * 256 : (m & 1) * 256 + 256], right, preferred_element_type=jnp.float32
                )
                if kx == 0 and m == 0:
                    total[...] = part
                else:
                    total[...] += part

    @pl.when(step == 3)
    def _():
        half = 0.5 * total[...]
        act = (half + half * jnp.tanh(half)).astype(jnp.bfloat16)
        for r in range(4):
            rows = slice(r * RUN, (r + 1) * RUN)
            u_ref[r] = act[rows, :DH]
            kv_ref[r, :, :DH] = act[rows, DH : 2 * DH]
            q_ref[r] = act[rows, 2 * DH : 3 * DH]
            kv_ref[r, :, DH:] = act[rows, 3 * DH :]


def attend_kernel(
    place,
    lengths,
    q_edges,
    k_edges,
    biases,
    q0,
    q1,
    q2,
    q3,
    kv_near,
    kv_far,
    q_ids,
    k_ids,
    table,
    send_ref,
    queries,
    acc,
):
    y, zl, core, zh = (place[i] for i in range(4))
    block = zl * 2 + core
    end0 = lengths[0]
    end1 = end0 + lengths[1]
    end2 = end1 + lengths[2]

    def user_start(pos):
        return jnp.where(
            pos >= end2, end2, jnp.where(pos >= end1, end1, jnp.where(pos >= end0, end0, 0))
        )

    for kz, source in enumerate((q0, q1, q2, q3)):
        rows = pl.ds(pl.multiple_of(((zh - kz) & 3) * RUN, RUN), RUN)
        for r in range(4):
            queries[r, rows, :] = source[r]
    table_rows = jnp.broadcast_to(table[...], (PAIR, DH))

    @pl.loop(0, 4)
    def _(r):
        group = (y - r) & 3
        first = group * 2048 + block * BLOCK
        start_low, start_high = user_start(first), user_start(first + BLOCK - 1)
        q_low, q_high = q_edges[r, 0], q_edges[r, 1]
        acc[...] = jnp.zeros_like(acc)

        def tile(t, carry):
            ky, zl_from = (y - (t >> 1)) & 3, t & 1
            zx = zl ^ zl_from
            near, far = kv_near[zx, ky], kv_far[zx, ky]
            keys = jnp.concatenate([near[:, DH:], far[:, DH:]], axis=0)
            values = jnp.concatenate([near[:, :DH], far[:, :DH]], axis=0)
            k_first = t * 1024 + zh * RUN
            k_last = k_first + BLOCK + RUN - 1
            gap_low = jnp.clip(q_low - k_edges[ky, zl_from * 2 + 1], 0, NB - 1)
            gap_high = jnp.clip(q_high - k_edges[ky, zl_from * 2], 0, NB - 1)
            plain = (k_last <= first) & (k_first >= start_high) & (gap_low == gap_high)

            def scores(part):
                rows = slice(part * PAIR, (part + 1) * PAIR)
                return rows, lax.dot_general(
                    queries[r, rows, :],
                    keys,
                    (((1,), (1,)), ((), ())),
                    preferred_element_type=jnp.float32,
                ) * (0.5 * SCALE)

            @pl.when(plain)
            def _():
                bias = 0.5 * biases[gap_low]
                for part in range(2):
                    rows, half = scores(part)
                    half = half + bias
                    weights = (half + half * jnp.tanh(half)).astype(jnp.bfloat16)
                    acc[rows, :] += jnp.dot(weights, values, preferred_element_type=jnp.float32)

            @pl.when(jnp.logical_not(plain))
            def _():
                k_row = k_ids[ky, pl.ds(zl_from, 1), :]
                column = lax.broadcasted_iota(jnp.int32, (1, PAIR), 1)
                k_pos = k_first + ((column >> 7) ^ core) * BLOCK + (column & (RUN - 1))
                for part in range(2):
                    rows, half = scores(part)
                    gaps = jnp.clip(q_ids[r, rows, :] - k_row, 0, NB - 1)
                    bias = jnp.concatenate(
                        [
                            jnp.take_along_axis(
                                table_rows,
                                gaps[:, c * DH : (c + 1) * DH],
                                axis=1,
                                mode="promise_in_bounds",
                            )
                            for c in range(PAIR // DH)
                        ],
                        axis=1,
                    )
                    half = half + 0.5 * bias
                    q_pos = first + part * PAIR + lax.broadcasted_iota(jnp.int32, (PAIR, 1), 0)
                    seen = (k_pos <= q_pos) & (k_pos >= user_start(q_pos))
                    silu = half + half * jnp.tanh(half)
                    weights = jnp.where(seen, silu, 0.0).astype(jnp.bfloat16)
                    acc[rows, :] += jnp.dot(weights, values, preferred_element_type=jnp.float32)

            return carry

        lowest = jnp.maximum((start_low - (BLOCK + RUN - 1) - zh * RUN + 1023) >> 10, 0)
        lax.fori_loop(lowest, group * 2 + zl + 1, tile, 0)
        attended = acc[...]
        centered = attended - jnp.mean(attended, axis=-1, keepdims=True)
        for zh_to in range(4):
            rows = slice(zh_to * RUN, (zh_to + 1) * RUN)
            send_ref[group * 4 + zh_to] = centered[rows, :].astype(jnp.bfloat16)


def gate_kernel(place, parts, u0, u1, u2, u3, gain, out_ref):
    y = place[0]
    for k, u in enumerate((u0, u1, u2, u3)):
        head = (y + k) & 3
        attended = parts[head * 4].astype(jnp.float32)
        for part in range(1, 4):
            attended += parts[head * 4 + part].astype(jnp.float32)
        mean = jnp.mean(attended, axis=-1, keepdims=True)
        centered = attended - mean
        var = jnp.mean(centered * centered, axis=-1, keepdims=True)
        normed = centered * lax.rsqrt(var + NORM_EPS) * gain[pl.ds(head, 1), :]
        columns = pl.ds(pl.multiple_of(head * DH, DH), DH)
        out_ref[:, columns] = (normed * u[...].astype(jnp.float32)).astype(jnp.bfloat16)


def output_kernel(place, tokens, gated, weights, out_ref):
    y, x = place[0], place[4]
    total = tokens[...].astype(jnp.float32)
    for ky in range(4):
        left = gated[(x - (y - ky)) & 3]
        right = jnp.concatenate([weights[j, 0, ky] for j in range(4)], axis=0)
        total += lax.dot_general(
            left, right, (((1,), (1,)), ((), ())), preferred_element_type=jnp.float32
        )
    out_ref[...] = total.astype(jnp.bfloat16)


def call(kernel, shapes, n_smem, n_vmem, scratch, flops, moved, vmem, name):
    return pl.pallas_call(
        kernel,
        out_shape=shapes,
        in_specs=[pl.BlockSpec(memory_space=pltpu.SMEM)] * n_smem
        + [pl.BlockSpec(memory_space=pltpu.VMEM)] * n_vmem,
        out_specs=jax.tree.map(lambda _: pl.BlockSpec(memory_space=pltpu.VMEM), shapes),
        scratch_shapes=scratch,
        compiler_params=pltpu.CompilerParams(vmem_limit_bytes=vmem * 2**20),
        cost_estimate=pl.CostEstimate(flops=flops, bytes_accessed=moved, transcendentals=0),
        name=name,
    )


def on_device(tokens, w_uvqk, w_out, rab_table, norm_gain, user_lengths, bucket_ids):
    bf16, f32 = jnp.bfloat16, jnp.float32
    y, zl, core, zh, x = (lax.axis_index(a) for a in ("y", "zl", "core", "zh", "x"))
    place = jnp.stack([y, zl, core, zh, x]).astype(jnp.int32)
    plane = ("zh", "zl", "core")

    ids = jnp.stack([bucket_ids // 128, bucket_ids % 128]).astype(bf16)
    ids = jnp.concatenate([ids, jnp.zeros((14, BLOCK), bf16)], axis=0)

    def columns(owner):
        part = lax.dynamic_slice_in_dim(w_uvqk, owner * 512, 512, 1)
        return jnp.concatenate([part, ids], axis=0)

    pieces = [columns(y)] + [
        lax.ppermute(columns((y + k) & 3), "y", [(i, (i + k) % 4) for i in range(4)])
        for k in range(1, 4)
    ]
    piece = jnp.stack(pieces)
    weights = lax.all_gather(piece, plane)

    first = rotations(tokens[:, :512], "y", 4)
    second = rotations(tokens[:, 512:], "x", 4)
    first, second = lax.optimization_barrier((first, second))
    firsts = rotations(jnp.concatenate(first, axis=0), "x", 4)
    seconds = rotations(jnp.concatenate(second, axis=0), "y", 4)

    late, _ = lax.optimization_barrier((w_out.T, piece))
    swapped = lax.ppermute(late, ("y", "x"), [(b * 4 + a, a * 4 + b) for a in range(4) for b in range(4)])
    swapped, firsts, seconds = lax.optimization_barrier((swapped, firsts, seconds))
    wo_rows = rotations(swapped, "y", 4)

    whole = pl.BlockSpec(memory_space=pltpu.VMEM)
    small = jax.ShapeDtypeStruct((4, RUN, DH), bf16)
    kv, q, u = pl.pallas_call(
        project_kernel,
        out_shape=[jax.ShapeDtypeStruct((4, RUN, 2 * DH), bf16), small, small],
        grid_spec=pltpu.PrefetchScalarGridSpec(
            num_scalar_prefetch=1,
            grid=(4,),
            in_specs=[whole] * 8
            + [pl.BlockSpec((16, 1, 80, 512), lambda i, p: (0, (p[0] - (p[4] - i)) & 3, 0, 0))],
            out_specs=[whole] * 3,
            scratch_shapes=[pltpu.VMEM((512, 512), f32)],
        ),
        compiler_params=pltpu.CompilerParams(vmem_limit_bytes=20 * 2**20),
        cost_estimate=pl.CostEstimate(
            flops=2 * 512 * 512 * 4096, bytes_accessed=9 * 2**20, transcendentals=0
        ),
        name="project",
    )(place, *firsts, *seconds, weights)

    wo_rows, _ = lax.optimization_barrier((wo_rows, kv))
    wo_all = lax.all_gather(jnp.stack(wo_rows), plane)

    q_all = rotations(q, "zh", 4)
    from_zl, q_all[1] = lax.optimization_barrier((swap(kv, "zl"), q_all[1]))
    kv_near = jnp.stack([kv, from_zl])
    kv_far = swap(kv_near, "core")

    coded = weights[:4, :, 64:66].astype(f32)
    all_ids = (coded[:, :, 0] * 128 + coded[:, :, 1]).astype(jnp.int32).transpose(1, 0, 2)
    q_ids = lax.dynamic_slice(all_ids, (0, zl * 2 + core, 0), (4, 1, BLOCK)).reshape(4, BLOCK, 1)
    q_edges = jnp.concatenate([q_ids[:, 0], q_ids[:, -1]], axis=1)
    k_ids = lax.dynamic_slice(all_ids, (0, 0, zh * RUN), (4, 4, RUN))
    k_edges = jnp.stack([k_ids[:, ::2, 0], k_ids[:, 1::2, -1]], axis=-1).reshape(4, 4)
    k_ids = k_ids.reshape(4, 2, 2, RUN)
    k_ids = jnp.where(core == 0, k_ids, k_ids[:, :, ::-1]).reshape(4, 2, PAIR)
    biases = lax.dynamic_slice(rab_table, (x * 4 + y, 0), (1, NB))
    gains = lax.dynamic_slice(norm_gain, (x * 4, 0), (4, DH))
    table = jnp.pad(biases, ((0, 0), (0, DH - NB)))

    parts = call(
        attend_kernel,
        jax.ShapeDtypeStruct((16, RUN, DH), bf16),
        5,
        9,
        [pltpu.VMEM((4, BLOCK, DH), bf16), pltpu.VMEM((BLOCK, DH), f32)],
        4 * 512 * 4096 * DH,
        5 * 2**20,
        14,
        "attend",
    )(place, user_lengths, q_edges, k_edges, biases[0], *q_all, kv_near, kv_far, q_ids, k_ids, table)

    u, _ = lax.optimization_barrier((u, (kv_far, q_all)))
    u_own = [u[0]] + [
        lax.ppermute(u[k], "y", [(i, (i - k) % 4) for i in range(4)]) for k in range(1, 4)
    ]
    arrived = lax.all_to_all(parts, ("y", "zh"), 0, 0, tiled=True)
    arrived, wo_all = lax.optimization_barrier((arrived, wo_all))
    gated = call(
        gate_kernel,
        jax.ShapeDtypeStruct((RUN, 4 * DH), bf16),
        1,
        6,
        [],
        20 * 512 * DH,
        2**20,
        4,
        "gate",
    )(place, arrived, *u_own, gains)
    heads = jnp.stack(rotations(gated, "x", 4))

    return pl.pallas_call(
        output_kernel,
        out_shape=jax.ShapeDtypeStruct((RUN, 1024), bf16),
        grid_spec=pltpu.PrefetchScalarGridSpec(
            num_scalar_prefetch=1,
            grid=(4,),
            in_specs=[
                pl.BlockSpec((RUN, 256), lambda i, p: (0, i)),
                whole,
                pl.BlockSpec((4, 1, 4, 64, 512), lambda i, p: (0, i, 0, 0, 0)),
            ],
            out_specs=pl.BlockSpec((RUN, 256), lambda i, p: (0, i)),
        ),
        compiler_params=pltpu.CompilerParams(vmem_limit_bytes=14 * 2**20),
        cost_estimate=pl.CostEstimate(
            flops=2 * RUN * 2048 * 1024, bytes_accessed=5 * 2**20, transcendentals=0
        ),
        name="project_out",
    )(place, tokens, heads, wo_all.reshape(4, 4, 4, 64, 512))


def solution(mesh):
    fine = Mesh(mesh.devices.reshape(4, 2, 2, 4, 4), ("y", "zl", "core", "zh", "x"))
    every = ("y", "zl", "core", "zh")
    placed = (
        P(every, "x"),
        P(every, "x"),
        P("x", every),
        P(),
        P(),
        P(),
        P(("y", "zl", "core")),
    )
    return jax.shard_map(
        on_device, mesh=fine, in_specs=placed, out_specs=P(every, "x"), check_vma=False
    )
```

```python
import functools

import jax
import jax.numpy as jnp
from jax import lax
from jax.experimental import pallas as pl
from jax.experimental.pallas import tpu as pltpu
from jax.sharding import Mesh
from jax.sharding import PartitionSpec as P

DH = 128
NB = 32
RUN = 128
BLOCK = 512
PAIR = 256
NORM_EPS = 1e-05
SCALE = DH ** (-0.5)


def rotations(value, axis, size, step=1):
    return [value] + [
        lax.ppermute(value, axis, [(i, (i + step * k) % size) for i in range(size)])
        for k in range(1, size)
    ]


def swap(value, axis):
    return lax.ppermute(value, axis, [(0, 1), (1, 0)])


def project_kernel(place, a0, a1, a2, a3, b0, b1, b2, b3, weights, kv_ref, q_ref, u_ref, total):
    step = pl.program_id(0)
    seconds = (b0, b1, b2, b3)
    for kx, first in enumerate((a0, a1, a2, a3)):

        @pl.when(step == kx)
        def _():
            second = jnp.concatenate([b[kx * RUN : (kx + 1) * RUN, :] for b in seconds], axis=0)
            for m in range(4):
                left = first[...] if m < 2 else second
                right = jnp.concatenate([weights[j * 4 + m, 0, :64, :] for j in range(4)], axis=0)
                part = jnp.dot(
                    left[:, (m & 1) * 256 : (m & 1) * 256 + 256], right, preferred_element_type=jnp.float32
                )
                if kx == 0 and m == 0:
                    total[...] = part
                else:
                    total[...] += part

    @pl.when(step == 3)
    def _():
        half = 0.5 * total[...]
        act = (half + half * jnp.tanh(half)).astype(jnp.bfloat16)
        for r in range(4):
            rows = slice(r * RUN, (r + 1) * RUN)
            u_ref[r] = act[rows, :DH]
            kv_ref[r, :, :DH] = act[rows, DH : 2 * DH]
            q_ref[r] = act[rows, 2 * DH : 3 * DH]
            kv_ref[r, :, DH:] = act[rows, 3 * DH :]


def attend_kernel(
    place,
    lengths,
    q_edges,
    k_edges,
    biases,
    q0,
    q1,
    q2,
    q3,
    kv_near,
    kv_far,
    q_ids,
    k_ids,
    table,
    send_ref,
    queries,
    acc,
):
    y, zl, core, zh = (place[i] for i in range(4))
    block = zl * 2 + core
    end0 = lengths[0]
    end1 = end0 + lengths[1]
    end2 = end1 + lengths[2]

    def user_start(pos):
        return jnp.where(
            pos >= end2, end2, jnp.where(pos >= end1, end1, jnp.where(pos >= end0, end0, 0))
        )

    for kz, source in enumerate((q0, q1, q2, q3)):
        rows = pl.ds(pl.multiple_of(((zh - kz) & 3) * RUN, RUN), RUN)
        for r in range(4):
            queries[r, rows, :] = source[r]
    table_rows = jnp.broadcast_to(table[...], (PAIR, DH))

    @pl.loop(0, 4)
    def _(r):
        group = (y - r) & 3
        first = group * 2048 + block * BLOCK
        start_low, start_high = user_start(first), user_start(first + BLOCK - 1)
        q_low, q_high = q_edges[r, 0], q_edges[r, 1]
        acc[...] = jnp.zeros_like(acc)

        def tile(t, carry):
            ky, zl_from = (y - (t >> 1)) & 3, t & 1
            zx = zl ^ zl_from
            near, far = kv_near[zx, ky], kv_far[zx, ky]
            keys = jnp.concatenate([near[:, DH:], far[:, DH:]], axis=0)
            values = jnp.concatenate([near[:, :DH], far[:, :DH]], axis=0)
            k_first = t * 1024 + zh * RUN
            k_last = k_first + BLOCK + RUN - 1
            gap_low = jnp.clip(q_low - k_edges[ky, zl_from * 2 + 1], 0, NB - 1)
            gap_high = jnp.clip(q_high - k_edges[ky, zl_from * 2], 0, NB - 1)
            plain = (k_last <= first) & (k_first >= start_high) & (gap_low == gap_high)

            def scores(part):
                rows = slice(part * PAIR, (part + 1) * PAIR)
                return rows, lax.dot_general(
                    queries[r, rows, :],
                    keys,
                    (((1,), (1,)), ((), ())),
                    preferred_element_type=jnp.float32,
                ) * (0.5 * SCALE)

            @pl.when(plain)
            def _():
                bias = 0.5 * biases[gap_low]
                for part in range(2):
                    rows, half = scores(part)
                    half = half + bias
                    weights = (half + half * jnp.tanh(half)).astype(jnp.bfloat16)
                    acc[rows, :] += jnp.dot(weights, values, preferred_element_type=jnp.float32)

            @pl.when(jnp.logical_not(plain))
            def _():
                k_row = k_ids[ky, pl.ds(zl_from, 1), :]
                column = lax.broadcasted_iota(jnp.int32, (1, PAIR), 1)
                k_pos = k_first + ((column >> 7) ^ core) * BLOCK + (column & (RUN - 1))
                for part in range(2):
                    rows, half = scores(part)
                    gaps = jnp.clip(q_ids[r, rows, :] - k_row, 0, NB - 1)
                    bias = jnp.concatenate(
                        [
                            jnp.take_along_axis(
                                table_rows,
                                gaps[:, c * DH : (c + 1) * DH],
                                axis=1,
                                mode="promise_in_bounds",
                            )
                            for c in range(PAIR // DH)
                        ],
                        axis=1,
                    )
                    half = half + 0.5 * bias
                    q_pos = first + part * PAIR + lax.broadcasted_iota(jnp.int32, (PAIR, 1), 0)
                    seen = (k_pos <= q_pos) & (k_pos >= user_start(q_pos))
                    silu = half + half * jnp.tanh(half)
                    weights = jnp.where(seen, silu, 0.0).astype(jnp.bfloat16)
                    acc[rows, :] += jnp.dot(weights, values, preferred_element_type=jnp.float32)

            return carry

        lowest = jnp.maximum((start_low - (BLOCK + RUN - 1) - zh * RUN + 1023) >> 10, 0)
        lax.fori_loop(lowest, group * 2 + zl + 1, tile, 0)
        attended = acc[...]
        centered = attended - jnp.mean(attended, axis=-1, keepdims=True)
        for zh_to in range(4):
            rows = slice(zh_to * RUN, (zh_to + 1) * RUN)
            send_ref[group * 4 + zh_to] = centered[rows, :].astype(jnp.bfloat16)


def gate_kernel(place, parts, u0, u1, u2, u3, gain, out_ref):
    y = place[0]
    for k, u in enumerate((u0, u1, u2, u3)):
        head = (y + k) & 3
        attended = parts[head * 4].astype(jnp.float32)
        for part in range(1, 4):
            attended += parts[head * 4 + part].astype(jnp.float32)
        mean = jnp.mean(attended, axis=-1, keepdims=True)
        centered = attended - mean
        var = jnp.mean(centered * centered, axis=-1, keepdims=True)
        normed = centered * lax.rsqrt(var + NORM_EPS) * gain[pl.ds(head, 1), :]
        columns = pl.ds(pl.multiple_of(head * DH, DH), DH)
        out_ref[:, columns] = (normed * u[...].astype(jnp.float32)).astype(jnp.bfloat16)


def output_kernel(place, tokens, gated, weights, out_ref):
    y, x = place[0], place[4]
    total = tokens[...].astype(jnp.float32)
    for ky in range(4):
        left = gated[(x - (y - ky)) & 3]
        right = jnp.concatenate([weights[j, 0, ky] for j in range(4)], axis=0)
        total += lax.dot_general(
            left, right, (((1,), (1,)), ((), ())), preferred_element_type=jnp.float32
        )
    out_ref[...] = total.astype(jnp.bfloat16)


def call(kernel, shapes, n_smem, n_vmem, scratch, flops, moved, vmem, name):
    return pl.pallas_call(
        kernel,
        out_shape=shapes,
        in_specs=[pl.BlockSpec(memory_space=pltpu.SMEM)] * n_smem
        + [pl.BlockSpec(memory_space=pltpu.VMEM)] * n_vmem,
        out_specs=jax.tree.map(lambda _: pl.BlockSpec(memory_space=pltpu.VMEM), shapes),
        scratch_shapes=scratch,
        compiler_params=pltpu.CompilerParams(vmem_limit_bytes=vmem * 2**20),
        cost_estimate=pl.CostEstimate(flops=flops, bytes_accessed=moved, transcendentals=0),
        name=name,
    )


def on_device(tokens, w_uvqk, w_out, rab_table, norm_gain, user_lengths, bucket_ids):
    bf16, f32 = jnp.bfloat16, jnp.float32
    y, zl, core, zh, x = (lax.axis_index(a) for a in ("y", "zl", "core", "zh", "x"))
    place = jnp.stack([y, zl, core, zh, x]).astype(jnp.int32)
    plane = ("zh", "zl", "core")

    ids = jnp.stack([bucket_ids // 128, bucket_ids % 128]).astype(bf16)
    ids = jnp.concatenate([ids, jnp.zeros((14, BLOCK), bf16)], axis=0)

    def columns(owner):
        part = lax.dynamic_slice_in_dim(w_uvqk, owner * 512, 512, 1)
        return jnp.concatenate([part, ids], axis=0)

    pieces = [columns(y)] + [
        lax.ppermute(columns((y + k) & 3), "y", [(i, (i + k) % 4) for i in range(4)])
        for k in range(1, 4)
    ]
    piece = jnp.stack(pieces)
    weights = lax.all_gather(piece, plane)

    late, _ = lax.optimization_barrier((w_out.T, piece))
    swapped = lax.ppermute(
        late, ("y", "x"), [(b * 4 + a, a * 4 + b) for a in range(4) for b in range(4)]
    )
    travelling, _ = lax.optimization_barrier((tokens, piece))

    first = rotations(travelling[:, :512], "y", 4)
    second = rotations(travelling[:, 512:], "x", 4)
    first, second, swapped = lax.optimization_barrier((first, second, swapped))
    firsts = rotations(jnp.concatenate(first, axis=0), "x", 4)
    seconds = rotations(jnp.concatenate(second, axis=0), "y", 4)

    swapped, firsts, seconds = lax.optimization_barrier((swapped, firsts, seconds))
    wo_rows = rotations(swapped, "y", 4)

    whole = pl.BlockSpec(memory_space=pltpu.VMEM)
    small = jax.ShapeDtypeStruct((4, RUN, DH), bf16)
    kv, q, u = pl.pallas_call(
        project_kernel,
        out_shape=[jax.ShapeDtypeStruct((4, RUN, 2 * DH), bf16), small, small],
        grid_spec=pltpu.PrefetchScalarGridSpec(
            num_scalar_prefetch=1,
            grid=(4,),
            in_specs=[whole] * 8
            + [pl.BlockSpec((16, 1, 80, 512), lambda i, p: (0, (p[0] - (p[4] - i)) & 3, 0, 0))],
            out_specs=[whole] * 3,
            scratch_shapes=[pltpu.VMEM((512, 512), f32)],
        ),
        compiler_params=pltpu.CompilerParams(vmem_limit_bytes=56 * 2**20),
        cost_estimate=pl.CostEstimate(
            flops=2 * 512 * 512 * 4096, bytes_accessed=9 * 2**20, transcendentals=0
        ),
        name="project",
    )(place, *firsts, *seconds, weights)

    wo_rows, _ = lax.optimization_barrier((wo_rows, kv))
    wo_all = lax.all_gather(jnp.stack(wo_rows), plane)

    q_all = rotations(q, "zh", 4)
    from_zl, q_all[1] = lax.optimization_barrier((swap(kv, "zl"), q_all[1]))
    kv_near = jnp.stack([kv, from_zl])
    kv_far = swap(kv_near, "core")

    coded = weights[:4, :, 64:66].astype(f32)
    all_ids = (coded[:, :, 0] * 128 + coded[:, :, 1]).astype(jnp.int32).transpose(1, 0, 2)
    q_ids = lax.dynamic_slice(all_ids, (0, zl * 2 + core, 0), (4, 1, BLOCK)).reshape(4, BLOCK, 1)
    q_edges = jnp.concatenate([q_ids[:, 0], q_ids[:, -1]], axis=1)
    k_ids = lax.dynamic_slice(all_ids, (0, 0, zh * RUN), (4, 4, RUN))
    k_edges = jnp.stack([k_ids[:, ::2, 0], k_ids[:, 1::2, -1]], axis=-1).reshape(4, 4)
    k_ids = k_ids.reshape(4, 2, 2, RUN)
    k_ids = jnp.where(core == 0, k_ids, k_ids[:, :, ::-1]).reshape(4, 2, PAIR)
    biases = lax.dynamic_slice(rab_table, (x * 4 + y, 0), (1, NB))
    gains = lax.dynamic_slice(norm_gain, (x * 4, 0), (4, DH))
    table = jnp.pad(biases, ((0, 0), (0, DH - NB)))

    parts = call(
        attend_kernel,
        jax.ShapeDtypeStruct((16, RUN, DH), bf16),
        5,
        9,
        [pltpu.VMEM((4, BLOCK, DH), bf16), pltpu.VMEM((BLOCK, DH), f32)],
        4 * 512 * 4096 * DH,
        5 * 2**20,
        14,
        "attend",
    )(place, user_lengths, q_edges, k_edges, biases[0], *q_all, kv_near, kv_far, q_ids, k_ids, table)

    u, _ = lax.optimization_barrier((u, (kv_far, q_all)))
    u_own = [u[0]] + [
        lax.ppermute(u[k], "y", [(i, (i - k) % 4) for i in range(4)]) for k in range(1, 4)
    ]
    arrived = lax.all_to_all(parts, ("y", "zh"), 0, 0, tiled=True)
    arrived, wo_all = lax.optimization_barrier((arrived, wo_all))
    gated = call(
        gate_kernel,
        jax.ShapeDtypeStruct((RUN, 4 * DH), bf16),
        1,
        6,
        [],
        20 * 512 * DH,
        2**20,
        4,
        "gate",
    )(place, arrived, *u_own, gains)
    heads = jnp.stack(rotations(gated, "x", 4))

    return pl.pallas_call(
        output_kernel,
        out_shape=jax.ShapeDtypeStruct((RUN, 1024), bf16),
        grid_spec=pltpu.PrefetchScalarGridSpec(
            num_scalar_prefetch=1,
            grid=(4,),
            in_specs=[
                pl.BlockSpec((RUN, 256), lambda i, p: (0, i)),
                whole,
                pl.BlockSpec((4, 1, 4, 64, 512), lambda i, p: (0, i, 0, 0, 0)),
            ],
            out_specs=pl.BlockSpec((RUN, 256), lambda i, p: (0, i)),
        ),
        compiler_params=pltpu.CompilerParams(vmem_limit_bytes=60 * 2**20),
        cost_estimate=pl.CostEstimate(
            flops=2 * RUN * 2048 * 1024, bytes_accessed=5 * 2**20, transcendentals=0
        ),
        name="project_out",
    )(place, tokens, heads, wo_all.reshape(4, 4, 4, 64, 512))


def solution(mesh):
    fine = Mesh(mesh.devices.reshape(4, 2, 2, 4, 4), ("y", "zl", "core", "zh", "x"))
    every = ("y", "zl", "core", "zh")
    placed = (
        P(every, "x"),
        P(every, "x"),
        P("x", every),
        P(),
        P(),
        P(),
        P(("y", "zl", "core")),
    )
    return jax.shard_map(
        on_device, mesh=fine, in_specs=placed, out_specs=P(every, "x"), check_vma=False
    )
```

```python
import functools

import jax
import jax.numpy as jnp
from jax import lax
from jax.experimental import pallas as pl
from jax.experimental.pallas import tpu as pltpu
from jax.sharding import Mesh
from jax.sharding import PartitionSpec as P

DH = 128
NB = 32
RUN = 128
BLOCK = 512
PAIR = 256
NORM_EPS = 1e-05
SCALE = DH ** (-0.5)


def rotations(value, axis, size, step=1):
    return [value] + [
        lax.ppermute(value, axis, [(i, (i + step * k) % size) for i in range(size)])
        for k in range(1, size)
    ]


def swap(value, axis):
    return lax.ppermute(value, axis, [(0, 1), (1, 0)])


def project_kernel(place, a0, a1, a2, a3, b0, b1, b2, b3, weights, kv_ref, q_ref, u_ref, total):
    y, x = place[0], place[4]
    seconds = (b0, b1, b2, b3)
    for kx, first in enumerate((a0, a1, a2, a3)):
        ky = (y - (x - kx)) & 3
        second = jnp.concatenate([b[kx * RUN : (kx + 1) * RUN, :] for b in seconds], axis=0)
        for m in range(4):
            left = first[...] if m < 2 else second
            right = jnp.concatenate([weights[j * 4 + m, ky, :64, :] for j in range(4)], axis=0)
            part = jnp.dot(
                left[:, (m & 1) * 256 : (m & 1) * 256 + 256], right, preferred_element_type=jnp.float32
            )
            if kx == 0 and m == 0:
                total[...] = part
            else:
                total[...] += part
    half = 0.5 * total[...]
    act = (half + half * jnp.tanh(half)).astype(jnp.bfloat16)
    for r in range(4):
        rows = slice(r * RUN, (r + 1) * RUN)
        u_ref[r] = act[rows, :DH]
        kv_ref[r, :, :DH] = act[rows, DH : 2 * DH]
        q_ref[r] = act[rows, 2 * DH : 3 * DH]
        kv_ref[r, :, DH:] = act[rows, 3 * DH :]


def attend_kernel(
    place,
    lengths,
    q_edges,
    k_edges,
    biases,
    q0,
    q1,
    q2,
    q3,
    kv_near,
    kv_far,
    q_ids,
    k_ids,
    table,
    send_ref,
    queries,
    acc,
):
    y, zl, core, zh = (place[i] for i in range(4))
    block = zl * 2 + core
    end0 = lengths[0]
    end1 = end0 + lengths[1]
    end2 = end1 + lengths[2]

    def user_start(pos):
        return jnp.where(
            pos >= end2, end2, jnp.where(pos >= end1, end1, jnp.where(pos >= end0, end0, 0))
        )

    for kz, source in enumerate((q0, q1, q2, q3)):
        rows = pl.ds(pl.multiple_of(((zh - kz) & 3) * RUN, RUN), RUN)
        for r in range(4):
            queries[r, rows, :] = source[r]
    table_rows = jnp.broadcast_to(table[...], (PAIR, DH))

    @pl.loop(0, 4)
    def _(r):
        group = (y - r) & 3
        first = group * 2048 + block * BLOCK
        start_low, start_high = user_start(first), user_start(first + BLOCK - 1)
        q_low, q_high = q_edges[r, 0], q_edges[r, 1]
        acc[...] = jnp.zeros_like(acc)

        def tile(t, carry):
            ky, zl_from = (y - (t >> 1)) & 3, t & 1
            zx = zl ^ zl_from
            near, far = kv_near[zx, ky], kv_far[zx, ky]
            keys = jnp.concatenate([near[:, DH:], far[:, DH:]], axis=0)
            values = jnp.concatenate([near[:, :DH], far[:, :DH]], axis=0)
            k_first = t * 1024 + zh * RUN
            k_last = k_first + BLOCK + RUN - 1
            gap_low = jnp.clip(q_low - k_edges[ky, zl_from * 2 + 1], 0, NB - 1)
            gap_high = jnp.clip(q_high - k_edges[ky, zl_from * 2], 0, NB - 1)
            plain = (k_last <= first) & (k_first >= start_high) & (gap_low == gap_high)

            def scores(part):
                rows = slice(part * PAIR, (part + 1) * PAIR)
                return rows, lax.dot_general(
                    queries[r, rows, :],
                    keys,
                    (((1,), (1,)), ((), ())),
                    preferred_element_type=jnp.float32,
                ) * (0.5 * SCALE)

            @pl.when(plain)
            def _():
                bias = 0.5 * biases[gap_low]
                for part in range(2):
                    rows, half = scores(part)
                    half = half + bias
                    weights = (half + half * jnp.tanh(half)).astype(jnp.bfloat16)
                    acc[rows, :] += jnp.dot(weights, values, preferred_element_type=jnp.float32)

            @pl.when(jnp.logical_not(plain))
            def _():
                k_row = k_ids[ky, pl.ds(zl_from, 1), :]
                column = lax.broadcasted_iota(jnp.int32, (1, PAIR), 1)
                k_pos = k_first + ((column >> 7) ^ core) * BLOCK + (column & (RUN - 1))
                for part in range(2):
                    rows, half = scores(part)
                    gaps = jnp.clip(q_ids[r, rows, :] - k_row, 0, NB - 1)
                    bias = jnp.concatenate(
                        [
                            jnp.take_along_axis(
                                table_rows,
                                gaps[:, c * DH : (c + 1) * DH],
                                axis=1,
                                mode="promise_in_bounds",
                            )
                            for c in range(PAIR // DH)
                        ],
                        axis=1,
                    )
                    half = half + 0.5 * bias
                    q_pos = first + part * PAIR + lax.broadcasted_iota(jnp.int32, (PAIR, 1), 0)
                    seen = (k_pos <= q_pos) & (k_pos >= user_start(q_pos))
                    silu = half + half * jnp.tanh(half)
                    weights = jnp.where(seen, silu, 0.0).astype(jnp.bfloat16)
                    acc[rows, :] += jnp.dot(weights, values, preferred_element_type=jnp.float32)

            return carry

        lowest = jnp.maximum((start_low - (BLOCK + RUN - 1) - zh * RUN + 1023) >> 10, 0)
        lax.fori_loop(lowest, group * 2 + zl + 1, tile, 0)
        attended = acc[...]
        centered = attended - jnp.mean(attended, axis=-1, keepdims=True)
        for zh_to in range(4):
            rows = slice(zh_to * RUN, (zh_to + 1) * RUN)
            send_ref[group * 4 + zh_to] = centered[rows, :].astype(jnp.bfloat16)


def gate_kernel(place, parts, u0, u1, u2, u3, gain, out_ref):
    y = place[0]
    for k, u in enumerate((u0, u1, u2, u3)):
        head = (y + k) & 3
        attended = parts[head * 4].astype(jnp.float32)
        for part in range(1, 4):
            attended += parts[head * 4 + part].astype(jnp.float32)
        mean = jnp.mean(attended, axis=-1, keepdims=True)
        centered = attended - mean
        var = jnp.mean(centered * centered, axis=-1, keepdims=True)
        normed = centered * lax.rsqrt(var + NORM_EPS) * gain[pl.ds(head, 1), :]
        columns = pl.ds(pl.multiple_of(head * DH, DH), DH)
        out_ref[:, columns] = (normed * u[...].astype(jnp.float32)).astype(jnp.bfloat16)


def output_kernel(place, tokens, gated, weights, out_ref):
    y, x = place[0], place[4]
    for m in range(4):
        columns = slice(m * 256, (m + 1) * 256)
        total = tokens[:, columns].astype(jnp.float32)
        for ky in range(4):
            left = gated[(x - (y - ky)) & 3]
            right = jnp.concatenate([weights[j * 4 + m, ky] for j in range(4)], axis=0)
            total += lax.dot_general(
                left, right, (((1,), (1,)), ((), ())), preferred_element_type=jnp.float32
            )
        out_ref[:, columns] = total.astype(jnp.bfloat16)


def call(kernel, shapes, n_smem, n_vmem, scratch, flops, moved, vmem, name):
    return pl.pallas_call(
        kernel,
        out_shape=shapes,
        in_specs=[pl.BlockSpec(memory_space=pltpu.SMEM)] * n_smem
        + [pl.BlockSpec(memory_space=pltpu.VMEM)] * n_vmem,
        out_specs=jax.tree.map(lambda _: pl.BlockSpec(memory_space=pltpu.VMEM), shapes),
        scratch_shapes=scratch,
        compiler_params=pltpu.CompilerParams(vmem_limit_bytes=vmem * 2**20),
        cost_estimate=pl.CostEstimate(flops=flops, bytes_accessed=moved, transcendentals=0),
        name=name,
    )


def on_device(tokens, w_uvqk, w_out, rab_table, norm_gain, user_lengths, bucket_ids):
    bf16, f32 = jnp.bfloat16, jnp.float32
    y, zl, core, zh, x = (lax.axis_index(a) for a in ("y", "zl", "core", "zh", "x"))
    place = jnp.stack([y, zl, core, zh, x]).astype(jnp.int32)
    plane = ("zh", "zl", "core")

    ids = jnp.stack([bucket_ids // 128, bucket_ids % 128]).astype(bf16)
    ids = jnp.concatenate([ids, jnp.zeros((14, BLOCK), bf16)], axis=0)

    def columns(owner):
        part = lax.dynamic_slice_in_dim(w_uvqk, owner * 512, 512, 1)
        return jnp.concatenate([part, ids], axis=0)

    pieces = [columns(y)] + [
        lax.ppermute(columns((y + k) & 3), "y", [(i, (i + k) % 4) for i in range(4)])
        for k in range(1, 4)
    ]
    piece = jnp.stack(pieces)
    weights = lax.all_gather(piece, plane)

    travelling, _ = lax.optimization_barrier((tokens, piece))

    first = rotations(travelling[:, :512], "y", 4)
    second = rotations(travelling[:, 512:], "x", 4)
    first, second = lax.optimization_barrier((first, second))
    firsts = rotations(jnp.concatenate(first, axis=0), "x", 4)
    seconds = rotations(jnp.concatenate(second, axis=0), "y", 4)

    late, firsts, seconds = lax.optimization_barrier((w_out.T, firsts, seconds))
    wo_rows = [
        lax.ppermute(
            late, ("y", "x"), [(b * 4 + a, (a + k) % 4 * 4 + b) for a in range(4) for b in range(4)]
        )
        for k in range(4)
    ]

    kv, q, u = call(
        project_kernel,
        [
            jax.ShapeDtypeStruct((4, RUN, 2 * DH), bf16),
            jax.ShapeDtypeStruct((4, RUN, DH), bf16),
            jax.ShapeDtypeStruct((4, RUN, DH), bf16),
        ],
        1,
        9,
        [pltpu.VMEM((512, 512), f32)],
        2 * 512 * 512 * 4096,
        9 * 2**20,
        24,
        "project",
    )(place, *firsts, *seconds, weights)

    wo_rows, _ = lax.optimization_barrier((wo_rows, kv))
    wo_all = lax.all_gather(jnp.stack(wo_rows), plane)

    kv_near = jnp.stack([kv, swap(kv, "zl")])
    kv_far = swap(kv_near, "core")
    q_all = rotations(q, "zh", 4)
    kv_far, q_all[1], q_all[2] = lax.optimization_barrier((kv_far, q_all[1], q_all[2]))

    coded = weights[:4, :, 64:66].astype(f32)
    all_ids = (coded[:, :, 0] * 128 + coded[:, :, 1]).astype(jnp.int32).transpose(1, 0, 2)
    q_ids = lax.dynamic_slice(all_ids, (0, zl * 2 + core, 0), (4, 1, BLOCK)).reshape(4, BLOCK, 1)
    q_edges = jnp.concatenate([q_ids[:, 0], q_ids[:, -1]], axis=1)
    k_ids = lax.dynamic_slice(all_ids, (0, 0, zh * RUN), (4, 4, RUN))
    k_edges = jnp.stack([k_ids[:, ::2, 0], k_ids[:, 1::2, -1]], axis=-1).reshape(4, 4)
    k_ids = k_ids.reshape(4, 2, 2, RUN)
    k_ids = jnp.where(core == 0, k_ids, k_ids[:, :, ::-1]).reshape(4, 2, PAIR)
    biases = lax.dynamic_slice(rab_table, (x * 4 + y, 0), (1, NB))
    gains = lax.dynamic_slice(norm_gain, (x * 4, 0), (4, DH))
    table = jnp.pad(biases, ((0, 0), (0, DH - NB)))

    parts = call(
        attend_kernel,
        jax.ShapeDtypeStruct((16, RUN, DH), bf16),
        5,
        9,
        [pltpu.VMEM((4, BLOCK, DH), bf16), pltpu.VMEM((BLOCK, DH), f32)],
        4 * 512 * 4096 * DH,
        5 * 2**20,
        14,
        "attend",
    )(place, user_lengths, q_edges, k_edges, biases[0], *q_all, kv_near, kv_far, q_ids, k_ids, table)

    u, _ = lax.optimization_barrier((u, (kv_far, q_all)))
    u_own = [u[0]] + [
        lax.ppermute(u[k], "y", [(i, (i - k) % 4) for i in range(4)]) for k in range(1, 4)
    ]
    arrived = lax.all_to_all(parts, ("y", "zh"), 0, 0, tiled=True)
    arrived, wo_all = lax.optimization_barrier((arrived, wo_all))
    gated = call(
        gate_kernel,
        jax.ShapeDtypeStruct((RUN, 4 * DH), bf16),
        1,
        6,
        [],
        20 * 512 * DH,
        2**20,
        4,
        "gate",
    )(place, arrived, *u_own, gains)
    heads = jnp.stack(rotations(gated, "x", 4))

    return call(
        output_kernel,
        jax.ShapeDtypeStruct((RUN, 1024), bf16),
        1,
        3,
        [],
        2 * RUN * 2048 * 1024,
        5 * 2**20,
        14,
        "project_out",
    )(place, tokens, heads, wo_all)


def solution(mesh):
    fine = Mesh(mesh.devices.reshape(4, 2, 2, 4, 4), ("y", "zl", "core", "zh", "x"))
    every = ("y", "zl", "core", "zh")
    placed = (
        P(every, "x"),
        P(every, "x"),
        P("x", every),
        P(),
        P(),
        P(),
        P(("y", "zl", "core")),
    )
    return jax.shard_map(
        on_device, mesh=fine, in_specs=placed, out_specs=P(every, "x"), check_vma=False
    )
```

```python
import functools

import jax
import jax.numpy as jnp
from jax import lax
from jax.experimental import pallas as pl
from jax.experimental.pallas import tpu as pltpu
from jax.sharding import Mesh
from jax.sharding import PartitionSpec as P

DH = 128
NB = 32
RUN = 128
BLOCK = 512
PAIR = 256
NORM_EPS = 1e-05
SCALE = DH ** (-0.5)


def rotations(value, axis, size, step=1):
    return [value] + [
        lax.ppermute(value, axis, [(i, (i + step * k) % size) for i in range(size)])
        for k in range(1, size)
    ]


def swap(value, axis):
    return lax.ppermute(value, axis, [(0, 1), (1, 0)])


def project_kernel(place, a0, a1, a2, a3, b0, b1, b2, b3, weights, kv_ref, q_ref, u_ref, total):
    y, x = place[0], place[4]
    seconds = (b0, b1, b2, b3)
    for kx, first in enumerate((a0, a1, a2, a3)):
        ky = (y - (x - kx)) & 3
        second = jnp.concatenate([b[kx * RUN : (kx + 1) * RUN, :] for b in seconds], axis=0)
        for m in range(4):
            left = first[...] if m < 2 else second
            right = jnp.concatenate([weights[j * 4 + m, ky, :64, :] for j in range(4)], axis=0)
            part = jnp.dot(
                left[:, (m & 1) * 256 : (m & 1) * 256 + 256], right, preferred_element_type=jnp.float32
            )
            if kx == 0 and m == 0:
                total[...] = part
            else:
                total[...] += part
    half = 0.5 * total[...]
    act = (half + half * jnp.tanh(half)).astype(jnp.bfloat16)
    for r in range(4):
        rows = slice(r * RUN, (r + 1) * RUN)
        u_ref[r] = act[rows, :DH]
        kv_ref[r, :, :DH] = act[rows, DH : 2 * DH]
        q_ref[r] = act[rows, 2 * DH : 3 * DH]
        kv_ref[r, :, DH:] = act[rows, 3 * DH :]


def attend_kernel(
    place,
    lengths,
    q_edges,
    k_edges,
    biases,
    q0,
    q1,
    q2,
    q3,
    kv_near,
    kv_far,
    q_ids,
    k_ids,
    table,
    send_ref,
    queries,
    acc,
):
    y, zl, core, zh = (place[i] for i in range(4))
    block = zl * 2 + core
    end0 = lengths[0]
    end1 = end0 + lengths[1]
    end2 = end1 + lengths[2]

    def user_start(pos):
        return jnp.where(
            pos >= end2, end2, jnp.where(pos >= end1, end1, jnp.where(pos >= end0, end0, 0))
        )

    for kz, source in enumerate((q0, q1, q2, q3)):
        rows = pl.ds(pl.multiple_of(((zh - kz) & 3) * RUN, RUN), RUN)
        for r in range(4):
            queries[r, rows, :] = source[r]
    table_rows = jnp.broadcast_to(table[...], (PAIR, DH))

    @pl.loop(0, 4)
    def _(r):
        group = (y - r) & 3
        first = group * 2048 + block * BLOCK
        start_low, start_high = user_start(first), user_start(first + BLOCK - 1)
        q_low, q_high = q_edges[r, 0], q_edges[r, 1]
        acc[...] = jnp.zeros_like(acc)

        def tile(t, carry):
            ky, zl_from = (y - (t >> 1)) & 3, t & 1
            zx = zl ^ zl_from
            near, far = kv_near[zx, ky], kv_far[zx, ky]
            keys = jnp.concatenate([near[:, DH:], far[:, DH:]], axis=0)
            values = jnp.concatenate([near[:, :DH], far[:, :DH]], axis=0)
            k_first = t * 1024 + zh * RUN
            k_last = k_first + BLOCK + RUN - 1
            gap_low = jnp.clip(q_low - k_edges[ky, zl_from * 2 + 1], 0, NB - 1)
            gap_high = jnp.clip(q_high - k_edges[ky, zl_from * 2], 0, NB - 1)
            plain = (k_last <= first) & (k_first >= start_high) & (gap_low == gap_high)

            def scores(part):
                rows = slice(part * PAIR, (part + 1) * PAIR)
                return rows, lax.dot_general(
                    queries[r, rows, :],
                    keys,
                    (((1,), (1,)), ((), ())),
                    preferred_element_type=jnp.float32,
                ) * (0.5 * SCALE)

            @pl.when(plain)
            def _():
                bias = 0.5 * biases[gap_low]
                for part in range(2):
                    rows, half = scores(part)
                    half = half + bias
                    weights = (half + half * jnp.tanh(half)).astype(jnp.bfloat16)
                    acc[rows, :] += jnp.dot(weights, values, preferred_element_type=jnp.float32)

            @pl.when(jnp.logical_not(plain))
            def _():
                k_row = k_ids[ky, pl.ds(zl_from, 1), :]
                column = lax.broadcasted_iota(jnp.int32, (1, PAIR), 1)
                k_pos = k_first + ((column >> 7) ^ core) * BLOCK + (column & (RUN - 1))
                for part in range(2):
                    rows, half = scores(part)
                    gaps = jnp.clip(q_ids[r, rows, :] - k_row, 0, NB - 1)
                    bias = jnp.concatenate(
                        [
                            jnp.take_along_axis(
                                table_rows,
                                gaps[:, c * DH : (c + 1) * DH],
                                axis=1,
                                mode="promise_in_bounds",
                            )
                            for c in range(PAIR // DH)
                        ],
                        axis=1,
                    )
                    half = half + 0.5 * bias
                    q_pos = first + part * PAIR + lax.broadcasted_iota(jnp.int32, (PAIR, 1), 0)
                    seen = (k_pos <= q_pos) & (k_pos >= user_start(q_pos))
                    silu = half + half * jnp.tanh(half)
                    weights = jnp.where(seen, silu, 0.0).astype(jnp.bfloat16)
                    acc[rows, :] += jnp.dot(weights, values, preferred_element_type=jnp.float32)

            return carry

        lowest = jnp.maximum((start_low - (BLOCK + RUN - 1) - zh * RUN + 1023) >> 10, 0)
        lax.fori_loop(lowest, group * 2 + zl + 1, tile, 0)
        attended = acc[...]
        centered = attended - jnp.mean(attended, axis=-1, keepdims=True)
        for zh_to in range(4):
            rows = slice(zh_to * RUN, (zh_to + 1) * RUN)
            send_ref[group * 4 + zh_to] = centered[rows, :].astype(jnp.bfloat16)


def gate_kernel(place, parts, u0, u1, u2, u3, gain, out_ref):
    y = place[0]
    for k, u in enumerate((u0, u1, u2, u3)):
        head = (y + k) & 3
        attended = parts[head * 4].astype(jnp.float32)
        for part in range(1, 4):
            attended += parts[head * 4 + part].astype(jnp.float32)
        mean = jnp.mean(attended, axis=-1, keepdims=True)
        centered = attended - mean
        var = jnp.mean(centered * centered, axis=-1, keepdims=True)
        normed = centered * lax.rsqrt(var + NORM_EPS) * gain[pl.ds(head, 1), :]
        columns = pl.ds(pl.multiple_of(head * DH, DH), DH)
        out_ref[:, columns] = (normed * u[...].astype(jnp.float32)).astype(jnp.bfloat16)


def output_kernel(place, gated, weights, own_ref, send_ref):
    y, x = place[0], place[4]
    for k in range(4):
        ky = (y - x - k) & 3
        for m in range(4):
            columns = slice(m * 256, (m + 1) * 256)
            right = jnp.concatenate([weights[j * 4 + m, ky] for j in range(4)], axis=0)
            part = lax.dot_general(
                gated[...], right, (((1,), (1,)), ((), ())), preferred_element_type=jnp.float32
            )
            if k == 0:
                own_ref[:, columns] = part
            else:
                send_ref[k - 1, :, columns] = part.astype(jnp.bfloat16)


def add_kernel(tokens, own, p1, p2, p3, out_ref):
    total = tokens[...].astype(jnp.float32) + own[...]
    for part in (p1, p2, p3):
        total += part[...].astype(jnp.float32)
    out_ref[...] = total.astype(jnp.bfloat16)


def call(kernel, shapes, n_smem, n_vmem, scratch, flops, moved, vmem, name):
    return pl.pallas_call(
        kernel,
        out_shape=shapes,
        in_specs=[pl.BlockSpec(memory_space=pltpu.SMEM)] * n_smem
        + [pl.BlockSpec(memory_space=pltpu.VMEM)] * n_vmem,
        out_specs=jax.tree.map(lambda _: pl.BlockSpec(memory_space=pltpu.VMEM), shapes),
        scratch_shapes=scratch,
        compiler_params=pltpu.CompilerParams(vmem_limit_bytes=vmem * 2**20),
        cost_estimate=pl.CostEstimate(flops=flops, bytes_accessed=moved, transcendentals=0),
        name=name,
    )


def on_device(tokens, w_uvqk, w_out, rab_table, norm_gain, user_lengths, bucket_ids):
    bf16, f32 = jnp.bfloat16, jnp.float32
    y, zl, core, zh, x = (lax.axis_index(a) for a in ("y", "zl", "core", "zh", "x"))
    place = jnp.stack([y, zl, core, zh, x]).astype(jnp.int32)
    plane = ("zh", "zl", "core")

    ids = jnp.stack([bucket_ids // 128, bucket_ids % 128]).astype(bf16)
    ids = jnp.concatenate([ids, jnp.zeros((14, BLOCK), bf16)], axis=0)

    def columns(owner):
        part = lax.dynamic_slice_in_dim(w_uvqk, owner * 512, 512, 1)
        return jnp.concatenate([part, ids], axis=0)

    pieces = [columns(y)] + [
        lax.ppermute(columns((y + k) & 3), "y", [(i, (i + k) % 4) for i in range(4)])
        for k in range(1, 4)
    ]
    piece = jnp.stack(pieces)
    weights = lax.all_gather(piece, plane)

    travelling, _ = lax.optimization_barrier((tokens, piece))

    first = rotations(jnp.concatenate([travelling[:, :512], w_out.T], axis=0), "y", 4)
    second = rotations(travelling[:, 512:], "x", 4)
    first, second = lax.optimization_barrier((first, second))
    firsts = rotations(jnp.concatenate([f[:RUN] for f in first], axis=0), "x", 4)
    seconds = rotations(jnp.concatenate(second, axis=0), "y", 4)
    wo_rows = jnp.stack([f[RUN:] for f in first])
    firsts, seconds, wo_rows = lax.optimization_barrier((firsts, seconds, wo_rows))

    kv, q, u = call(
        project_kernel,
        [
            jax.ShapeDtypeStruct((4, RUN, 2 * DH), bf16),
            jax.ShapeDtypeStruct((4, RUN, DH), bf16),
            jax.ShapeDtypeStruct((4, RUN, DH), bf16),
        ],
        1,
        9,
        [pltpu.VMEM((512, 512), f32)],
        2 * 512 * 512 * 4096,
        9 * 2**20,
        24,
        "project",
    )(place, *firsts, *seconds, weights)

    wo_rows, _ = lax.optimization_barrier((wo_rows, weights))
    wo_all = lax.all_gather(wo_rows, plane)

    kv_near = jnp.stack([kv, swap(kv, "zl")])
    kv_far = swap(kv_near, "core")
    q_all = rotations(q, "zh", 4)
    kv_far, q_all[1], q_all[2] = lax.optimization_barrier((kv_far, q_all[1], q_all[2]))

    coded = weights[:4, :, 64:66].astype(f32)
    all_ids = (coded[:, :, 0] * 128 + coded[:, :, 1]).astype(jnp.int32).transpose(1, 0, 2)
    q_ids = lax.dynamic_slice(all_ids, (0, zl * 2 + core, 0), (4, 1, BLOCK)).reshape(4, BLOCK, 1)
    q_edges = jnp.concatenate([q_ids[:, 0], q_ids[:, -1]], axis=1)
    k_ids = lax.dynamic_slice(all_ids, (0, 0, zh * RUN), (4, 4, RUN))
    k_edges = jnp.stack([k_ids[:, ::2, 0], k_ids[:, 1::2, -1]], axis=-1).reshape(4, 4)
    k_ids = k_ids.reshape(4, 2, 2, RUN)
    k_ids = jnp.where(core == 0, k_ids, k_ids[:, :, ::-1]).reshape(4, 2, PAIR)
    biases = lax.dynamic_slice(rab_table, (x * 4 + y, 0), (1, NB))
    gains = lax.dynamic_slice(norm_gain, (x * 4, 0), (4, DH))
    table = jnp.pad(biases, ((0, 0), (0, DH - NB)))

    parts = call(
        attend_kernel,
        jax.ShapeDtypeStruct((16, RUN, DH), bf16),
        5,
        9,
        [pltpu.VMEM((4, BLOCK, DH), bf16), pltpu.VMEM((BLOCK, DH), f32)],
        4 * 512 * 4096 * DH,
        5 * 2**20,
        14,
        "attend",
    )(place, user_lengths, q_edges, k_edges, biases[0], *q_all, kv_near, kv_far, q_ids, k_ids, table)

    u, _ = lax.optimization_barrier((u, (kv_far, q_all)))
    u_own = [u[0]] + [
        lax.ppermute(u[k], "y", [(i, (i - k) % 4) for i in range(4)]) for k in range(1, 4)
    ]
    arrived = lax.all_to_all(parts, ("y", "zh"), 0, 0, tiled=True)
    arrived, wo_all = lax.optimization_barrier((arrived, wo_all))
    gated = call(
        gate_kernel,
        jax.ShapeDtypeStruct((RUN, 4 * DH), bf16),
        1,
        6,
        [],
        20 * 512 * DH,
        2**20,
        4,
        "gate",
    )(place, arrived, *u_own, gains)
    own, shares = call(
        output_kernel,
        [jax.ShapeDtypeStruct((RUN, 1024), f32), jax.ShapeDtypeStruct((3, RUN, 1024), bf16)],
        1,
        2,
        [],
        2 * RUN * 512 * 4096,
        5 * 2**20,
        14,
        "project_out",
    )(place, gated, wo_all)
    shares = [
        lax.ppermute(shares[k - 1], "x", [(i, (i + k) % 4) for i in range(4)]) for k in range(1, 4)
    ]
    return call(
        add_kernel,
        jax.ShapeDtypeStruct((RUN, 1024), bf16),
        0,
        5,
        [],
        5 * RUN * 1024,
        2**20,
        8,
        "add",
    )(tokens, own, *shares)


def solution(mesh):
    fine = Mesh(mesh.devices.reshape(4, 2, 2, 4, 4), ("y", "zl", "core", "zh", "x"))
    every = ("y", "zl", "core", "zh")
    placed = (
        P(every, "x"),
        P(every, "x"),
        P("x", every),
        P(),
        P(),
        P(),
        P(("y", "zl", "core")),
    )
    return jax.shard_map(
        on_device, mesh=fine, in_specs=placed, out_specs=P(every, "x"), check_vma=False
    )
```

```python
import functools

import jax
import jax.numpy as jnp
from jax import lax
from jax.experimental import pallas as pl
from jax.experimental.pallas import tpu as pltpu
from jax.sharding import Mesh
from jax.sharding import PartitionSpec as P

DH = 128
NB = 32
RUN = 128
BLOCK = 512
PAIR = 256
NORM_EPS = 1e-05
SCALE = DH ** (-0.5)


def rotations(value, axis, size, step=1):
    return [value] + [
        lax.ppermute(value, axis, [(i, (i + step * k) % size) for i in range(size)])
        for k in range(1, size)
    ]


def swap(value, axis):
    return lax.ppermute(value, axis, [(0, 1), (1, 0)])


def project_kernel(place, a0, a1, a2, a3, b0, b1, b2, b3, weights, kv_ref, q_ref, u_ref, total):
    y, x = place[0], place[4]
    seconds = (b0, b1, b2, b3)
    for kx, first in enumerate((a0, a1, a2, a3)):
        ky = (y - (x - kx)) & 3
        second = jnp.concatenate([b[kx * RUN : (kx + 1) * RUN, :] for b in seconds], axis=0)
        for m in range(4):
            left = first[...] if m < 2 else second
            right = jnp.concatenate([weights[j * 4 + m, ky, :64, :] for j in range(4)], axis=0)
            part = jnp.dot(
                left[:, (m & 1) * 256 : (m & 1) * 256 + 256], right, preferred_element_type=jnp.float32
            )
            if kx == 0 and m == 0:
                total[...] = part
            else:
                total[...] += part
    half = 0.5 * total[...]
    act = (half + half * jnp.tanh(half)).astype(jnp.bfloat16)
    for r in range(4):
        rows = slice(r * RUN, (r + 1) * RUN)
        u_ref[r] = act[rows, :DH]
        kv_ref[r, :, :DH] = act[rows, DH : 2 * DH]
        q_ref[r] = act[rows, 2 * DH : 3 * DH]
        kv_ref[r, :, DH:] = act[rows, 3 * DH :]


def attend_kernel(
    place,
    lengths,
    q_edges,
    k_edges,
    biases,
    q0,
    q1,
    q2,
    q3,
    kv_near,
    kv_far,
    q_ids,
    k_ids,
    table,
    send_ref,
    queries,
    acc,
):
    y, zl, core, zh = (place[i] for i in range(4))
    block = zl * 2 + core
    end0 = lengths[0]
    end1 = end0 + lengths[1]
    end2 = end1 + lengths[2]

    def user_start(pos):
        return jnp.where(
            pos >= end2, end2, jnp.where(pos >= end1, end1, jnp.where(pos >= end0, end0, 0))
        )

    for kz, source in enumerate((q0, q1, q2, q3)):
        rows = pl.ds(pl.multiple_of(((zh - kz) & 3) * RUN, RUN), RUN)
        for r in range(4):
            queries[r, rows, :] = source[r]
    table_rows = jnp.broadcast_to(table[...], (PAIR, DH))

    @pl.loop(0, 4)
    def _(r):
        group = (y - r) & 3
        first = group * 2048 + block * BLOCK
        start_low, start_high = user_start(first), user_start(first + BLOCK - 1)
        q_low, q_high = q_edges[r, 0], q_edges[r, 1]
        acc[...] = jnp.zeros_like(acc)

        def tile(t, carry):
            ky, zl_from = (y - (t >> 1)) & 3, t & 1
            zx = zl ^ zl_from
            near, far = kv_near[zx, ky], kv_far[zx, ky]
            keys = jnp.concatenate([near[:, DH:], far[:, DH:]], axis=0)
            values = jnp.concatenate([near[:, :DH], far[:, :DH]], axis=0)
            k_first = t * 1024 + zh * RUN
            k_last = k_first + BLOCK + RUN - 1
            gap_low = jnp.clip(q_low - k_edges[ky, zl_from * 2 + 1], 0, NB - 1)
            gap_high = jnp.clip(q_high - k_edges[ky, zl_from * 2], 0, NB - 1)
            plain = (k_last <= first) & (k_first >= start_high) & (gap_low == gap_high)

            def scores(part):
                rows = slice(part * PAIR, (part + 1) * PAIR)
                return rows, lax.dot_general(
                    queries[r, rows, :],
                    keys,
                    (((1,), (1,)), ((), ())),
                    preferred_element_type=jnp.float32,
                ) * (0.5 * SCALE)

            @pl.when(plain)
            def _():
                bias = 0.5 * biases[gap_low]
                for part in range(2):
                    rows, half = scores(part)
                    half = half + bias
                    weights = (half + half * jnp.tanh(half)).astype(jnp.bfloat16)
                    acc[rows, :] += jnp.dot(weights, values, preferred_element_type=jnp.float32)

            @pl.when(jnp.logical_not(plain))
            def _():
                k_row = k_ids[ky, pl.ds(zl_from, 1), :]
                column = lax.broadcasted_iota(jnp.int32, (1, PAIR), 1)
                k_pos = k_first + ((column >> 7) ^ core) * BLOCK + (column & (RUN - 1))
                for part in range(2):
                    rows, half = scores(part)
                    gaps = jnp.clip(q_ids[r, rows, :] - k_row, 0, NB - 1)
                    bias = jnp.concatenate(
                        [
                            jnp.take_along_axis(
                                table_rows,
                                gaps[:, c * DH : (c + 1) * DH],
                                axis=1,
                                mode="promise_in_bounds",
                            )
                            for c in range(PAIR // DH)
                        ],
                        axis=1,
                    )
                    half = half + 0.5 * bias
                    q_pos = first + part * PAIR + lax.broadcasted_iota(jnp.int32, (PAIR, 1), 0)
                    seen = (k_pos <= q_pos) & (k_pos >= user_start(q_pos))
                    silu = half + half * jnp.tanh(half)
                    weights = jnp.where(seen, silu, 0.0).astype(jnp.bfloat16)
                    acc[rows, :] += jnp.dot(weights, values, preferred_element_type=jnp.float32)

            return carry

        lowest = jnp.maximum((start_low - (BLOCK + RUN - 1) - zh * RUN + 1023) >> 10, 0)
        lax.fori_loop(lowest, group * 2 + zl + 1, tile, 0)
        attended = acc[...]
        centered = attended - jnp.mean(attended, axis=-1, keepdims=True)
        for zh_to in range(4):
            rows = slice(zh_to * RUN, (zh_to + 1) * RUN)
            send_ref[group * 4 + zh_to] = centered[rows, :].astype(jnp.bfloat16)


def gate_kernel(place, parts, u0, u1, u2, u3, gain, out_ref):
    y = place[0]
    for k, u in enumerate((u0, u1, u2, u3)):
        head = (y + k) & 3
        attended = parts[head * 4].astype(jnp.float32)
        for part in range(1, 4):
            attended += parts[head * 4 + part].astype(jnp.float32)
        mean = jnp.mean(attended, axis=-1, keepdims=True)
        centered = attended - mean
        var = jnp.mean(centered * centered, axis=-1, keepdims=True)
        normed = centered * lax.rsqrt(var + NORM_EPS) * gain[pl.ds(head, 1), :]
        columns = pl.ds(pl.multiple_of(head * DH, DH), DH)
        out_ref[:, columns] = (normed * u[...].astype(jnp.float32)).astype(jnp.bfloat16)


def output_kernel(place, tokens, gated, weights, out_ref):
    y, x = place[0], place[4]
    for m in range(4):
        columns = slice(m * 256, (m + 1) * 256)
        total = tokens[:, columns].astype(jnp.float32)
        for ky in range(4):
            left = gated[(x - (y - ky)) & 3]
            right = jnp.concatenate([weights[j * 4 + m, ky] for j in range(4)], axis=0)
            total += lax.dot_general(
                left, right, (((1,), (1,)), ((), ())), preferred_element_type=jnp.float32
            )
        out_ref[:, columns] = total.astype(jnp.bfloat16)


def call(kernel, shapes, n_smem, n_vmem, scratch, flops, moved, vmem, name):
    return pl.pallas_call(
        kernel,
        out_shape=shapes,
        in_specs=[pl.BlockSpec(memory_space=pltpu.SMEM)] * n_smem
        + [pl.BlockSpec(memory_space=pltpu.VMEM)] * n_vmem,
        out_specs=jax.tree.map(lambda _: pl.BlockSpec(memory_space=pltpu.VMEM), shapes),
        scratch_shapes=scratch,
        compiler_params=pltpu.CompilerParams(vmem_limit_bytes=vmem * 2**20),
        cost_estimate=pl.CostEstimate(flops=flops, bytes_accessed=moved, transcendentals=0),
        name=name,
    )


def on_device(tokens, w_uvqk, w_out, rab_table, norm_gain, user_lengths, bucket_ids):
    bf16, f32 = jnp.bfloat16, jnp.float32
    y, zl, core, zh, x = (lax.axis_index(a) for a in ("y", "zl", "core", "zh", "x"))
    place = jnp.stack([y, zl, core, zh, x]).astype(jnp.int32)
    plane = ("zh", "zl", "core")

    ids = jnp.stack([bucket_ids // 128, bucket_ids % 128]).astype(bf16)
    ids = jnp.concatenate([ids, jnp.zeros((14, BLOCK), bf16)], axis=0)

    def columns(owner):
        part = lax.dynamic_slice_in_dim(w_uvqk, owner * 512, 512, 1)
        return jnp.concatenate([part, ids], axis=0)

    pieces = [columns(y)] + [
        lax.ppermute(columns((y + k) & 3), "y", [(i, (i + k) % 4) for i in range(4)])
        for k in range(1, 4)
    ]
    swapped = lax.ppermute(
        w_out.T, ("y", "x"), [(b * 4 + a, a * 4 + b) for a in range(4) for b in range(4)]
    )
    pieces, swapped = lax.optimization_barrier((pieces, swapped))
    piece = jnp.stack(pieces)
    weights = lax.all_gather(piece, plane)

    travelling, _ = lax.optimization_barrier((tokens, piece))

    first = rotations(jnp.concatenate([travelling[:, :512], swapped], axis=0), "y", 4)
    second = rotations(travelling[:, 512:], "x", 4)
    first, second = lax.optimization_barrier((first, second))
    firsts = rotations(jnp.concatenate([f[:RUN] for f in first], axis=0), "x", 4)
    seconds = rotations(jnp.concatenate(second, axis=0), "y", 4)
    wo_rows = jnp.stack([f[RUN:] for f in first])
    firsts, seconds, wo_rows = lax.optimization_barrier((firsts, seconds, wo_rows))

    kv, q, u = call(
        project_kernel,
        [
            jax.ShapeDtypeStruct((4, RUN, 2 * DH), bf16),
            jax.ShapeDtypeStruct((4, RUN, DH), bf16),
            jax.ShapeDtypeStruct((4, RUN, DH), bf16),
        ],
        1,
        9,
        [pltpu.VMEM((512, 512), f32)],
        2 * 512 * 512 * 4096,
        9 * 2**20,
        24,
        "project",
    )(place, *firsts, *seconds, weights)

    wo_rows, _ = lax.optimization_barrier((wo_rows, weights))
    wo_all = lax.all_gather(wo_rows, plane)

    from_zl = swap(kv, "zl")
    later, from_zl = lax.optimization_barrier((q, from_zl))
    kv_near = jnp.stack([kv, from_zl])
    kv_far = swap(kv_near, "core")
    q_all = [q] + [
        lax.ppermute(q if k == 1 else later, "zh", [(i, (i + k) % 4) for i in range(4)])
        for k in range(1, 4)
    ]

    coded = weights[:4, :, 64:66].astype(f32)
    all_ids = (coded[:, :, 0] * 128 + coded[:, :, 1]).astype(jnp.int32).transpose(1, 0, 2)
    q_ids = lax.dynamic_slice(all_ids, (0, zl * 2 + core, 0), (4, 1, BLOCK)).reshape(4, BLOCK, 1)
    q_edges = jnp.concatenate([q_ids[:, 0], q_ids[:, -1]], axis=1)
    k_ids = lax.dynamic_slice(all_ids, (0, 0, zh * RUN), (4, 4, RUN))
    k_edges = jnp.stack([k_ids[:, ::2, 0], k_ids[:, 1::2, -1]], axis=-1).reshape(4, 4)
    k_ids = k_ids.reshape(4, 2, 2, RUN)
    k_ids = jnp.where(core == 0, k_ids, k_ids[:, :, ::-1]).reshape(4, 2, PAIR)
    biases = lax.dynamic_slice(rab_table, (x * 4 + y, 0), (1, NB))
    gains = lax.dynamic_slice(norm_gain, (x * 4, 0), (4, DH))
    table = jnp.pad(biases, ((0, 0), (0, DH - NB)))

    parts = call(
        attend_kernel,
        jax.ShapeDtypeStruct((16, RUN, DH), bf16),
        5,
        9,
        [pltpu.VMEM((4, BLOCK, DH), bf16), pltpu.VMEM((BLOCK, DH), f32)],
        4 * 512 * 4096 * DH,
        5 * 2**20,
        14,
        "attend",
    )(place, user_lengths, q_edges, k_edges, biases[0], *q_all, kv_near, kv_far, q_ids, k_ids, table)

    u, _ = lax.optimization_barrier((u, (kv_far, q_all)))
    u_own = [u[0]] + [
        lax.ppermute(u[k], "y", [(i, (i - k) % 4) for i in range(4)]) for k in range(1, 4)
    ]
    arrived = lax.all_to_all(parts, ("y", "zh"), 0, 0, tiled=True)
    arrived, wo_all = lax.optimization_barrier((arrived, wo_all))
    gated = call(
        gate_kernel,
        jax.ShapeDtypeStruct((RUN, 4 * DH), bf16),
        1,
        6,
        [],
        20 * 512 * DH,
        2**20,
        4,
        "gate",
    )(place, arrived, *u_own, gains)
    heads = jnp.stack(rotations(gated, "x", 4))

    return call(
        output_kernel,
        jax.ShapeDtypeStruct((RUN, 1024), bf16),
        1,
        3,
        [],
        2 * RUN * 2048 * 1024,
        5 * 2**20,
        14,
        "project_out",
    )(place, tokens, heads, wo_all)


def solution(mesh):
    fine = Mesh(mesh.devices.reshape(4, 2, 2, 4, 4), ("y", "zl", "core", "zh", "x"))
    every = ("y", "zl", "core", "zh")
    placed = (
        P(every, "x"),
        P(every, "x"),
        P("x", every),
        P(),
        P(),
        P(),
        P(("y", "zl", "core")),
    )
    return jax.shard_map(
        on_device, mesh=fine, in_specs=placed, out_specs=P(every, "x"), check_vma=False
    )
```

```python
import functools

import jax
import jax.numpy as jnp
from jax import lax
from jax.experimental import pallas as pl
from jax.experimental.pallas import tpu as pltpu
from jax.sharding import Mesh
from jax.sharding import PartitionSpec as P

DH = 128
NB = 32
RUN = 128
BLOCK = 512
PAIR = 256
NORM_EPS = 1e-05
SCALE = DH ** (-0.5)


def rotations(value, axis, size, step=1):
    return [value] + [
        lax.ppermute(value, axis, [(i, (i + step * k) % size) for i in range(size)])
        for k in range(1, size)
    ]


def swap(value, axis):
    return lax.ppermute(value, axis, [(0, 1), (1, 0)])


def project_kernel(place, a0, a1, a2, a3, b0, b1, b2, b3, weights, kv_ref, q_ref, u_ref, total):
    y, x = place[0], place[4]
    seconds = (b0, b1, b2, b3)
    for kx, first in enumerate((a0, a1, a2, a3)):
        ky = (y - (x - kx)) & 3
        second = jnp.concatenate([b[kx * RUN : (kx + 1) * RUN, :] for b in seconds], axis=0)
        for m in range(4):
            left = first[...] if m < 2 else second
            right = jnp.concatenate([weights[j * 4 + m, ky, :64, :] for j in range(4)], axis=0)
            part = jnp.dot(
                left[:, (m & 1) * 256 : (m & 1) * 256 + 256], right, preferred_element_type=jnp.float32
            )
            if kx == 0 and m == 0:
                total[...] = part
            else:
                total[...] += part
    half = 0.5 * total[...]
    act = (half + half * jnp.tanh(half)).astype(jnp.bfloat16)
    for r in range(4):
        rows = slice(r * RUN, (r + 1) * RUN)
        u_ref[r] = act[rows, :DH]
        kv_ref[r, :, :DH] = act[rows, DH : 2 * DH]
        q_ref[r] = act[rows, 2 * DH : 3 * DH]
        kv_ref[r, :, DH:] = act[rows, 3 * DH :]


def attend_kernel(
    place,
    lengths,
    q_edges,
    k_edges,
    biases,
    q0,
    q1,
    q2,
    q3,
    kv_near,
    kv_far,
    q_ids,
    k_ids,
    table,
    send_ref,
    queries,
    acc,
):
    y, zl, core, zh = (place[i] for i in range(4))
    block = zl * 2 + core
    end0 = lengths[0]
    end1 = end0 + lengths[1]
    end2 = end1 + lengths[2]

    def user_start(pos):
        return jnp.where(
            pos >= end2, end2, jnp.where(pos >= end1, end1, jnp.where(pos >= end0, end0, 0))
        )

    for kz, source in enumerate((q0, q1, q2, q3)):
        rows = pl.ds(pl.multiple_of(((zh - kz) & 3) * RUN, RUN), RUN)
        for r in range(4):
            queries[r, rows, :] = source[r]
    table_rows = jnp.broadcast_to(table[...], (PAIR, DH))

    @pl.loop(0, 4)
    def _(r):
        group = (y - r) & 3
        first = group * 2048 + block * BLOCK
        start_low, start_high = user_start(first), user_start(first + BLOCK - 1)
        q_low, q_high = q_edges[r, 0], q_edges[r, 1]
        acc[...] = jnp.zeros_like(acc)

        def tile(t, carry):
            ky, zl_from = (y - (t >> 1)) & 3, t & 1
            zx = zl ^ zl_from
            near, far = kv_near[zx, ky], kv_far[zx, ky]
            keys = jnp.concatenate([near[:, DH:], far[:, DH:]], axis=0)
            values = jnp.concatenate([near[:, :DH], far[:, :DH]], axis=0)
            k_first = t * 1024 + zh * RUN
            k_last = k_first + BLOCK + RUN - 1
            gap_low = jnp.clip(q_low - k_edges[ky, zl_from * 2 + 1], 0, NB - 1)
            gap_high = jnp.clip(q_high - k_edges[ky, zl_from * 2], 0, NB - 1)
            plain = (k_last <= first) & (k_first >= start_high) & (gap_low == gap_high)

            def scores(part):
                rows = slice(part * PAIR, (part + 1) * PAIR)
                return rows, lax.dot_general(
                    queries[r, rows, :],
                    keys,
                    (((1,), (1,)), ((), ())),
                    preferred_element_type=jnp.float32,
                ) * (0.5 * SCALE)

            @pl.when(plain)
            def _():
                bias = 0.5 * biases[gap_low]
                for part in range(2):
                    rows, half = scores(part)
                    half = half + bias
                    weights = (half + half * jnp.tanh(half)).astype(jnp.bfloat16)
                    acc[rows, :] += jnp.dot(weights, values, preferred_element_type=jnp.float32)

            @pl.when(jnp.logical_not(plain))
            def _():
                k_row = k_ids[ky, pl.ds(zl_from, 1), :]
                column = lax.broadcasted_iota(jnp.int32, (1, PAIR), 1)
                k_pos = k_first + ((column >> 7) ^ core) * BLOCK + (column & (RUN - 1))
                for part in range(2):
                    rows, half = scores(part)
                    gaps = jnp.clip(q_ids[r, rows, :] - k_row, 0, NB - 1)
                    bias = jnp.concatenate(
                        [
                            jnp.take_along_axis(
                                table_rows,
                                gaps[:, c * DH : (c + 1) * DH],
                                axis=1,
                                mode="promise_in_bounds",
                            )
                            for c in range(PAIR // DH)
                        ],
                        axis=1,
                    )
                    half = half + 0.5 * bias
                    q_pos = first + part * PAIR + lax.broadcasted_iota(jnp.int32, (PAIR, 1), 0)
                    seen = (k_pos <= q_pos) & (k_pos >= user_start(q_pos))
                    silu = half + half * jnp.tanh(half)
                    weights = jnp.where(seen, silu, 0.0).astype(jnp.bfloat16)
                    acc[rows, :] += jnp.dot(weights, values, preferred_element_type=jnp.float32)

            return carry

        lowest = jnp.maximum((start_low - (BLOCK + RUN - 1) - zh * RUN + 1023) >> 10, 0)
        lax.fori_loop(lowest, group * 2 + zl + 1, tile, 0)
        attended = acc[...]
        centered = attended - jnp.mean(attended, axis=-1, keepdims=True)
        for zh_to in range(4):
            rows = slice(zh_to * RUN, (zh_to + 1) * RUN)
            send_ref[group * 4 + zh_to] = centered[rows, :].astype(jnp.bfloat16)


def gate_kernel(place, parts, u0, u1, u2, u3, gain, out_ref):
    y = place[0]
    for k, u in enumerate((u0, u1, u2, u3)):
        head = (y + k) & 3
        attended = parts[head * 4].astype(jnp.float32)
        for part in range(1, 4):
            attended += parts[head * 4 + part].astype(jnp.float32)
        mean = jnp.mean(attended, axis=-1, keepdims=True)
        centered = attended - mean
        var = jnp.mean(centered * centered, axis=-1, keepdims=True)
        normed = centered * lax.rsqrt(var + NORM_EPS) * gain[pl.ds(head, 1), :]
        columns = pl.ds(pl.multiple_of(head * DH, DH), DH)
        out_ref[:, columns] = (normed * u[...].astype(jnp.float32)).astype(jnp.bfloat16)


def output_kernel(place, tokens, gated, weights, out_ref):
    y, x = place[0], place[4]
    for m in range(4):
        columns = slice(m * 256, (m + 1) * 256)
        total = tokens[:, columns].astype(jnp.float32)
        for ky in range(4):
            left = gated[(x - (y - ky)) & 3]
            right = jnp.concatenate([weights[j * 4 + m, ky] for j in range(4)], axis=0)
            total += lax.dot_general(
                left, right, (((1,), (1,)), ((), ())), preferred_element_type=jnp.float32
            )
        out_ref[:, columns] = total.astype(jnp.bfloat16)


def call(kernel, shapes, n_smem, n_vmem, scratch, flops, moved, vmem, name):
    return pl.pallas_call(
        kernel,
        out_shape=shapes,
        in_specs=[pl.BlockSpec(memory_space=pltpu.SMEM)] * n_smem
        + [pl.BlockSpec(memory_space=pltpu.VMEM)] * n_vmem,
        out_specs=jax.tree.map(lambda _: pl.BlockSpec(memory_space=pltpu.VMEM), shapes),
        scratch_shapes=scratch,
        compiler_params=pltpu.CompilerParams(vmem_limit_bytes=vmem * 2**20),
        cost_estimate=pl.CostEstimate(flops=flops, bytes_accessed=moved, transcendentals=0),
        name=name,
    )


def on_device(tokens, w_uvqk, w_out, rab_table, norm_gain, user_lengths, bucket_ids):
    bf16, f32 = jnp.bfloat16, jnp.float32
    y, zl, core, zh, x = (lax.axis_index(a) for a in ("y", "zl", "core", "zh", "x"))
    place = jnp.stack([y, zl, core, zh, x]).astype(jnp.int32)
    plane = ("zh", "zl", "core")

    ids = jnp.stack([bucket_ids // 128, bucket_ids % 128]).astype(bf16)
    ids = jnp.concatenate([ids, jnp.zeros((14, BLOCK), bf16)], axis=0)

    def columns(owner):
        part = lax.dynamic_slice_in_dim(w_uvqk, owner * 512, 512, 1)
        return jnp.concatenate([part, ids], axis=0)

    pieces = [columns(y)] + [
        lax.ppermute(columns((y + k) & 3), "y", [(i, (i + k) % 4) for i in range(4)])
        for k in range(1, 4)
    ]
    piece = jnp.stack(pieces)
    weights = lax.all_gather(piece, plane)

    travelling, _ = lax.optimization_barrier((tokens, piece))

    first = rotations(travelling[:, :512], "y", 4)
    second = rotations(travelling[:, 512:], "x", 4)
    first, second = lax.optimization_barrier((first, second))
    firsts = rotations(jnp.concatenate(first, axis=0), "x", 4)
    seconds = rotations(jnp.concatenate(second, axis=0), "y", 4)

    kv, q, u = call(
        project_kernel,
        [
            jax.ShapeDtypeStruct((4, RUN, 2 * DH), bf16),
            jax.ShapeDtypeStruct((4, RUN, DH), bf16),
            jax.ShapeDtypeStruct((4, RUN, DH), bf16),
        ],
        1,
        9,
        [pltpu.VMEM((512, 512), f32)],
        2 * 512 * 512 * 4096,
        9 * 2**20,
        24,
        "project",
    )(place, *firsts, *seconds, weights)

    from_zl = swap(kv, "zl")
    kv_near = jnp.stack([kv, from_zl])
    kv_far = swap(kv_near, "core")
    q_all = rotations(q, "zh", 4)
    kv_far, q_all[1], q_all[2] = lax.optimization_barrier((kv_far, q_all[1], q_all[2]))

    late, _ = lax.optimization_barrier((w_out.T, from_zl))
    wo_rows = [
        lax.ppermute(
            late, ("y", "x"), [(b * 4 + a, (a + k) % 4 * 4 + b) for a in range(4) for b in range(4)]
        )
        for k in range(4)
    ]
    wo_rows, kv_far, q_all = lax.optimization_barrier((wo_rows, kv_far, q_all))
    wo_all = lax.all_gather(jnp.stack(wo_rows), plane)

    coded = weights[:4, :, 64:66].astype(f32)
    all_ids = (coded[:, :, 0] * 128 + coded[:, :, 1]).astype(jnp.int32).transpose(1, 0, 2)
    q_ids = lax.dynamic_slice(all_ids, (0, zl * 2 + core, 0), (4, 1, BLOCK)).reshape(4, BLOCK, 1)
    q_edges = jnp.concatenate([q_ids[:, 0], q_ids[:, -1]], axis=1)
    k_ids = lax.dynamic_slice(all_ids, (0, 0, zh * RUN), (4, 4, RUN))
    k_edges = jnp.stack([k_ids[:, ::2, 0], k_ids[:, 1::2, -1]], axis=-1).reshape(4, 4)
    k_ids = k_ids.reshape(4, 2, 2, RUN)
    k_ids = jnp.where(core == 0, k_ids, k_ids[:, :, ::-1]).reshape(4, 2, PAIR)
    biases = lax.dynamic_slice(rab_table, (x * 4 + y, 0), (1, NB))
    gains = lax.dynamic_slice(norm_gain, (x * 4, 0), (4, DH))
    table = jnp.pad(biases, ((0, 0), (0, DH - NB)))

    parts = call(
        attend_kernel,
        jax.ShapeDtypeStruct((16, RUN, DH), bf16),
        5,
        9,
        [pltpu.VMEM((4, BLOCK, DH), bf16), pltpu.VMEM((BLOCK, DH), f32)],
        4 * 512 * 4096 * DH,
        5 * 2**20,
        14,
        "attend",
    )(place, user_lengths, q_edges, k_edges, biases[0], *q_all, kv_near, kv_far, q_ids, k_ids, table)

    u, _ = lax.optimization_barrier((u, (kv_far, q_all)))
    u_own = [u[0]] + [
        lax.ppermute(u[k], "y", [(i, (i - k) % 4) for i in range(4)]) for k in range(1, 4)
    ]
    arrived = lax.all_to_all(parts, ("y", "zh"), 0, 0, tiled=True)
    gated = call(
        gate_kernel,
        jax.ShapeDtypeStruct((RUN, 4 * DH), bf16),
        1,
        6,
        [],
        20 * 512 * DH,
        2**20,
        4,
        "gate",
    )(place, arrived, *u_own, gains)
    heads = jnp.stack(rotations(gated, "x", 4))

    return call(
        output_kernel,
        jax.ShapeDtypeStruct((RUN, 1024), bf16),
        1,
        3,
        [],
        2 * RUN * 2048 * 1024,
        5 * 2**20,
        14,
        "project_out",
    )(place, tokens, heads, wo_all)


def solution(mesh):
    fine = Mesh(mesh.devices.reshape(4, 2, 2, 4, 4), ("y", "zl", "core", "zh", "x"))
    every = ("y", "zl", "core", "zh")
    placed = (
        P(every, "x"),
        P(every, "x"),
        P("x", every),
        P(),
        P(),
        P(),
        P(("y", "zl", "core")),
    )
    return jax.shard_map(
        on_device, mesh=fine, in_specs=placed, out_specs=P(every, "x"), check_vma=False
    )
```

```python
import functools

import jax
import jax.numpy as jnp
from jax import lax
from jax.experimental import pallas as pl
from jax.experimental.pallas import tpu as pltpu
from jax.sharding import Mesh
from jax.sharding import PartitionSpec as P

DH = 128
NB = 32
RUN = 128
BLOCK = 512
PAIR = 256
NORM_EPS = 1e-05
SCALE = DH ** (-0.5)


def rotations(value, axis, size, step=1):
    return [value] + [
        lax.ppermute(value, axis, [(i, (i + step * k) % size) for i in range(size)])
        for k in range(1, size)
    ]


def swap(value, axis):
    return lax.ppermute(value, axis, [(0, 1), (1, 0)])


def project_kernel(place, a0, a1, a2, a3, b0, b1, b2, b3, weights, kv_ref, q_ref, u_ref, total):
    y, x = place[0], place[4]
    seconds = (b0, b1, b2, b3)
    for kx, first in enumerate((a0, a1, a2, a3)):
        ky = (y - (x - kx)) & 3
        second = jnp.concatenate([b[kx * RUN : (kx + 1) * RUN, :] for b in seconds], axis=0)
        for m in range(4):
            left = first[...] if m < 2 else second
            right = jnp.concatenate([weights[j * 4 + m, ky, :64, :] for j in range(4)], axis=0)
            part = jnp.dot(
                left[:, (m & 1) * 256 : (m & 1) * 256 + 256], right, preferred_element_type=jnp.float32
            )
            if kx == 0 and m == 0:
                total[...] = part
            else:
                total[...] += part
    half = 0.5 * total[...]
    act = (half + half * jnp.tanh(half)).astype(jnp.bfloat16)
    for r in range(4):
        rows = slice(r * RUN, (r + 1) * RUN)
        u_ref[r] = act[rows, :DH]
        kv_ref[r, :, :DH] = act[rows, DH : 2 * DH]
        q_ref[r] = act[rows, 2 * DH : 3 * DH]
        kv_ref[r, :, DH:] = act[rows, 3 * DH :]


def attend_kernel(
    place,
    lengths,
    q_edges,
    k_edges,
    biases,
    q0,
    q1,
    q2,
    q3,
    kv_near,
    kv_far,
    q_ids,
    k_ids,
    table,
    send_ref,
    queries,
    acc,
):
    y, zl, core, zh = (place[i] for i in range(4))
    block = zl * 2 + core
    end0 = lengths[0]
    end1 = end0 + lengths[1]
    end2 = end1 + lengths[2]

    def user_start(pos):
        return jnp.where(
            pos >= end2, end2, jnp.where(pos >= end1, end1, jnp.where(pos >= end0, end0, 0))
        )

    for kz, source in enumerate((q0, q1, q2, q3)):
        rows = pl.ds(pl.multiple_of(((zh - kz) & 3) * RUN, RUN), RUN)
        for r in range(4):
            queries[r, rows, :] = source[r]
    table_rows = jnp.broadcast_to(table[...], (PAIR, DH))

    @pl.loop(0, 4)
    def _(r):
        group = (y - r) & 3
        first = group * 2048 + block * BLOCK
        start_low, start_high = user_start(first), user_start(first + BLOCK - 1)
        q_low, q_high = q_edges[r, 0], q_edges[r, 1]
        acc[...] = jnp.zeros_like(acc)

        def tile(t, carry):
            ky, zl_from = (y - (t >> 1)) & 3, t & 1
            zx = zl ^ zl_from
            near, far = kv_near[zx, ky], kv_far[zx, ky]
            keys = jnp.concatenate([near[:, DH:], far[:, DH:]], axis=0)
            values = jnp.concatenate([near[:, :DH], far[:, :DH]], axis=0)
            k_first = t * 1024 + zh * RUN
            k_last = k_first + BLOCK + RUN - 1
            gap_low = jnp.clip(q_low - k_edges[ky, zl_from * 2 + 1], 0, NB - 1)
            gap_high = jnp.clip(q_high - k_edges[ky, zl_from * 2], 0, NB - 1)
            plain = (k_last <= first) & (k_first >= start_high) & (gap_low == gap_high)

            def scores(part):
                rows = slice(part * PAIR, (part + 1) * PAIR)
                return rows, lax.dot_general(
                    queries[r, rows, :],
                    keys,
                    (((1,), (1,)), ((), ())),
                    preferred_element_type=jnp.float32,
                ) * (0.5 * SCALE)

            @pl.when(plain)
            def _():
                bias = 0.5 * biases[gap_low]
                for part in range(2):
                    rows, half = scores(part)
                    half = half + bias
                    weights = (half + half * jnp.tanh(half)).astype(jnp.bfloat16)
                    acc[rows, :] += jnp.dot(weights, values, preferred_element_type=jnp.float32)

            @pl.when(jnp.logical_not(plain))
            def _():
                k_row = k_ids[ky, pl.ds(zl_from, 1), :]
                column = lax.broadcasted_iota(jnp.int32, (1, PAIR), 1)
                k_pos = k_first + ((column >> 7) ^ core) * BLOCK + (column & (RUN - 1))
                for part in range(2):
                    rows, half = scores(part)
                    gaps = jnp.clip(q_ids[r, rows, :] - k_row, 0, NB - 1)
                    bias = jnp.concatenate(
                        [
                            jnp.take_along_axis(
                                table_rows,
                                gaps[:, c * DH : (c + 1) * DH],
                                axis=1,
                                mode="promise_in_bounds",
                            )
                            for c in range(PAIR // DH)
                        ],
                        axis=1,
                    )
                    half = half + 0.5 * bias
                    q_pos = first + part * PAIR + lax.broadcasted_iota(jnp.int32, (PAIR, 1), 0)
                    seen = (k_pos <= q_pos) & (k_pos >= user_start(q_pos))
                    silu = half + half * jnp.tanh(half)
                    weights = jnp.where(seen, silu, 0.0).astype(jnp.bfloat16)
                    acc[rows, :] += jnp.dot(weights, values, preferred_element_type=jnp.float32)

            return carry

        lowest = jnp.maximum((start_low - (BLOCK + RUN - 1) - zh * RUN + 1023) >> 10, 0)
        lax.fori_loop(lowest, group * 2 + zl + 1, tile, 0)
        attended = acc[...]
        centered = attended - jnp.mean(attended, axis=-1, keepdims=True)
        for zh_to in range(4):
            rows = slice(zh_to * RUN, (zh_to + 1) * RUN)
            send_ref[group * 4 + zh_to] = centered[rows, :].astype(jnp.bfloat16)


def finish_kernel(place, parts, u0, u1, u2, u3, gain, weights, own_ref, send_ref, gated):
    y, x = place[0], place[4]
    for k, u in enumerate((u0, u1, u2, u3)):
        head = (y + k) & 3
        attended = parts[head * 4].astype(jnp.float32)
        for part in range(1, 4):
            attended += parts[head * 4 + part].astype(jnp.float32)
        mean = jnp.mean(attended, axis=-1, keepdims=True)
        centered = attended - mean
        var = jnp.mean(centered * centered, axis=-1, keepdims=True)
        normed = centered * lax.rsqrt(var + NORM_EPS) * gain[pl.ds(head, 1), :]
        columns = pl.ds(pl.multiple_of(head * DH, DH), DH)
        gated[:, columns] = (normed * u[...].astype(jnp.float32)).astype(jnp.bfloat16)
    for k in range(4):
        ky = (y - x - k) & 3
        for m in range(4):
            columns = slice(m * 256, (m + 1) * 256)
            right = jnp.concatenate([weights[j * 4 + m, ky] for j in range(4)], axis=0)
            part = lax.dot_general(
                gated[...], right, (((1,), (1,)), ((), ())), preferred_element_type=jnp.float32
            )
            if k == 0:
                own_ref[:, columns] = part
            else:
                send_ref[k - 1, :, columns] = part.astype(jnp.bfloat16)


def add_kernel(tokens, own, p1, p2, p3, out_ref):
    total = tokens[...].astype(jnp.float32) + own[...]
    for part in (p1, p2, p3):
        total += part[...].astype(jnp.float32)
    out_ref[...] = total.astype(jnp.bfloat16)


def call(kernel, shapes, n_smem, n_vmem, scratch, flops, moved, vmem, name):
    return pl.pallas_call(
        kernel,
        out_shape=shapes,
        in_specs=[pl.BlockSpec(memory_space=pltpu.SMEM)] * n_smem
        + [pl.BlockSpec(memory_space=pltpu.VMEM)] * n_vmem,
        out_specs=jax.tree.map(lambda _: pl.BlockSpec(memory_space=pltpu.VMEM), shapes),
        scratch_shapes=scratch,
        compiler_params=pltpu.CompilerParams(vmem_limit_bytes=vmem * 2**20),
        cost_estimate=pl.CostEstimate(flops=flops, bytes_accessed=moved, transcendentals=0),
        name=name,
    )


def on_device(tokens, w_uvqk, w_out, rab_table, norm_gain, user_lengths, bucket_ids):
    bf16, f32 = jnp.bfloat16, jnp.float32
    y, zl, core, zh, x = (lax.axis_index(a) for a in ("y", "zl", "core", "zh", "x"))
    place = jnp.stack([y, zl, core, zh, x]).astype(jnp.int32)
    plane = ("zh", "zl", "core")

    ids = jnp.stack([bucket_ids // 128, bucket_ids % 128]).astype(bf16)
    ids = jnp.concatenate([ids, jnp.zeros((14, BLOCK), bf16)], axis=0)

    def columns(owner):
        part = lax.dynamic_slice_in_dim(w_uvqk, owner * 512, 512, 1)
        return jnp.concatenate([part, ids], axis=0)

    pieces = [columns(y)] + [
        lax.ppermute(columns((y + k) & 3), "y", [(i, (i + k) % 4) for i in range(4)])
        for k in range(1, 4)
    ]
    piece = jnp.stack(pieces)
    weights = lax.all_gather(piece, plane)

    travelling, _ = lax.optimization_barrier((tokens, piece))

    first = rotations(jnp.concatenate([travelling[:, :512], w_out.T], axis=0), "y", 4)
    second = rotations(travelling[:, 512:], "x", 4)
    first, second = lax.optimization_barrier((first, second))
    firsts = rotations(jnp.concatenate([f[:RUN] for f in first], axis=0), "x", 4)
    seconds = rotations(jnp.concatenate(second, axis=0), "y", 4)
    wo_rows = jnp.stack([f[RUN:] for f in first])
    firsts, seconds, wo_rows = lax.optimization_barrier((firsts, seconds, wo_rows))

    kv, q, u = call(
        project_kernel,
        [
            jax.ShapeDtypeStruct((4, RUN, 2 * DH), bf16),
            jax.ShapeDtypeStruct((4, RUN, DH), bf16),
            jax.ShapeDtypeStruct((4, RUN, DH), bf16),
        ],
        1,
        9,
        [pltpu.VMEM((512, 512), f32)],
        2 * 512 * 512 * 4096,
        9 * 2**20,
        24,
        "project",
    )(place, *firsts, *seconds, weights)

    wo_rows, _ = lax.optimization_barrier((wo_rows, weights))
    wo_all = lax.all_gather(wo_rows, plane)

    from_zl = swap(kv, "zl")
    later, from_zl = lax.optimization_barrier((q, from_zl))
    kv_near = jnp.stack([kv, from_zl])
    kv_far = swap(kv_near, "core")
    q_all = [q] + [
        lax.ppermute(q if k == 1 else later, "zh", [(i, (i + k) % 4) for i in range(4)])
        for k in range(1, 4)
    ]

    coded = weights[:4, :, 64:66].astype(f32)
    all_ids = (coded[:, :, 0] * 128 + coded[:, :, 1]).astype(jnp.int32).transpose(1, 0, 2)
    q_ids = lax.dynamic_slice(all_ids, (0, zl * 2 + core, 0), (4, 1, BLOCK)).reshape(4, BLOCK, 1)
    q_edges = jnp.concatenate([q_ids[:, 0], q_ids[:, -1]], axis=1)
    k_ids = lax.dynamic_slice(all_ids, (0, 0, zh * RUN), (4, 4, RUN))
    k_edges = jnp.stack([k_ids[:, ::2, 0], k_ids[:, 1::2, -1]], axis=-1).reshape(4, 4)
    k_ids = k_ids.reshape(4, 2, 2, RUN)
    k_ids = jnp.where(core == 0, k_ids, k_ids[:, :, ::-1]).reshape(4, 2, PAIR)
    biases = lax.dynamic_slice(rab_table, (x * 4 + y, 0), (1, NB))
    gains = lax.dynamic_slice(norm_gain, (x * 4, 0), (4, DH))
    table = jnp.pad(biases, ((0, 0), (0, DH - NB)))

    parts = call(
        attend_kernel,
        jax.ShapeDtypeStruct((16, RUN, DH), bf16),
        5,
        9,
        [pltpu.VMEM((4, BLOCK, DH), bf16), pltpu.VMEM((BLOCK, DH), f32)],
        4 * 512 * 4096 * DH,
        5 * 2**20,
        14,
        "attend",
    )(place, user_lengths, q_edges, k_edges, biases[0], *q_all, kv_near, kv_far, q_ids, k_ids, table)

    u, _ = lax.optimization_barrier((u, (kv_far, q_all)))
    u_own = [u[0]] + [
        lax.ppermute(u[k], "y", [(i, (i - k) % 4) for i in range(4)]) for k in range(1, 4)
    ]
    arrived = lax.all_to_all(parts, ("y", "zh"), 0, 0, tiled=True)
    arrived, wo_all = lax.optimization_barrier((arrived, wo_all))
    own, shares = call(
        finish_kernel,
        [jax.ShapeDtypeStruct((RUN, 1024), f32), jax.ShapeDtypeStruct((3, RUN, 1024), bf16)],
        1,
        7,
        [pltpu.VMEM((RUN, 4 * DH), bf16)],
        2 * RUN * 512 * 4096,
        5 * 2**20,
        14,
        "finish",
    )(place, arrived, *u_own, gains, wo_all)
    shares = [
        lax.ppermute(shares[k - 1], "x", [(i, (i + k) % 4) for i in range(4)]) for k in range(1, 4)
    ]
    return call(
        add_kernel,
        jax.ShapeDtypeStruct((RUN, 1024), bf16),
        0,
        5,
        [],
        5 * RUN * 1024,
        2**20,
        8,
        "add",
    )(tokens, own, *shares)


def solution(mesh):
    fine = Mesh(mesh.devices.reshape(4, 2, 2, 4, 4), ("y", "zl", "core", "zh", "x"))
    every = ("y", "zl", "core", "zh")
    placed = (
        P(every, "x"),
        P(every, "x"),
        P("x", every),
        P(),
        P(),
        P(),
        P(("y", "zl", "core")),
    )
    return jax.shard_map(
        on_device, mesh=fine, in_specs=placed, out_specs=P(every, "x"), check_vma=False
    )
```

```python
import functools

import jax
import jax.numpy as jnp
from jax import lax
from jax.experimental import pallas as pl
from jax.experimental.pallas import tpu as pltpu
from jax.sharding import Mesh
from jax.sharding import PartitionSpec as P

DH = 128
NB = 32
RUN = 128
BLOCK = 512
PAIR = 256
NORM_EPS = 1e-05
SCALE = DH ** (-0.5)


def rotations(value, axis, size, step=1):
    return [value] + [
        lax.ppermute(value, axis, [(i, (i + step * k) % size) for i in range(size)])
        for k in range(1, size)
    ]


def swap(value, axis):
    return lax.ppermute(value, axis, [(0, 1), (1, 0)])


def project_kernel(low, place, a0, a1, a2, a3, b0, b1, b2, b3, weights, *outs):
    *out_refs, total = outs
    y, x = place[0], place[4]
    seconds = (b0, b1, b2, b3)
    for kx, first in enumerate((a0, a1, a2, a3)):
        ky = (y - (x - kx)) & 3
        second = jnp.concatenate([b[kx * RUN : (kx + 1) * RUN, :] for b in seconds], axis=0)
        for m in range(4):
            left = first[...] if m < 2 else second
            rows = [weights[j * 4 + m, ky, :64, :] for j in range(4)]
            right = jnp.concatenate(
                [
                    jnp.concatenate([r[:, c : c + DH] for r in rows], axis=0)
                    for c in (low, low + 2 * DH)
                ],
                axis=1,
            )
            part = jnp.dot(
                left[:, (m & 1) * 256 : (m & 1) * 256 + 256], right, preferred_element_type=jnp.float32
            )
            if kx == 0 and m == 0:
                total[...] = part
            else:
                total[...] += part
    half = 0.5 * total[...]
    act = (half + half * jnp.tanh(half)).astype(jnp.bfloat16)
    for r in range(4):
        rows = slice(r * RUN, (r + 1) * RUN)
        if len(out_refs) == 1:
            out_refs[0][r] = act[rows, :]
        else:
            out_refs[0][r] = act[rows, :DH]
            out_refs[1][r] = act[rows, DH:]


def attend_kernel(
    place,
    lengths,
    q_edges,
    k_edges,
    biases,
    q0,
    q1,
    q2,
    q3,
    kv_near,
    kv_far,
    q_ids,
    k_ids,
    table,
    send_ref,
    queries,
    acc,
):
    y, zl, core, zh = (place[i] for i in range(4))
    block = zl * 2 + core
    end0 = lengths[0]
    end1 = end0 + lengths[1]
    end2 = end1 + lengths[2]

    def user_start(pos):
        return jnp.where(
            pos >= end2, end2, jnp.where(pos >= end1, end1, jnp.where(pos >= end0, end0, 0))
        )

    for kz, source in enumerate((q0, q1, q2, q3)):
        rows = pl.ds(pl.multiple_of(((zh - kz) & 3) * RUN, RUN), RUN)
        for r in range(4):
            queries[r, rows, :] = source[r]
    table_rows = jnp.broadcast_to(table[...], (PAIR, DH))

    @pl.loop(0, 4)
    def _(r):
        group = (y - r) & 3
        first = group * 2048 + block * BLOCK
        start_low, start_high = user_start(first), user_start(first + BLOCK - 1)
        q_low, q_high = q_edges[r, 0], q_edges[r, 1]
        acc[...] = jnp.zeros_like(acc)

        def tile(t, carry):
            ky, zl_from = (y - (t >> 1)) & 3, t & 1
            zx = zl ^ zl_from
            near, far = kv_near[zx, ky], kv_far[zx, ky]
            keys = jnp.concatenate([near[:, DH:], far[:, DH:]], axis=0)
            values = jnp.concatenate([near[:, :DH], far[:, :DH]], axis=0)
            k_first = t * 1024 + zh * RUN
            k_last = k_first + BLOCK + RUN - 1
            gap_low = jnp.clip(q_low - k_edges[ky, zl_from * 2 + 1], 0, NB - 1)
            gap_high = jnp.clip(q_high - k_edges[ky, zl_from * 2], 0, NB - 1)
            plain = (k_last <= first) & (k_first >= start_high) & (gap_low == gap_high)

            def scores(part):
                rows = slice(part * PAIR, (part + 1) * PAIR)
                return rows, lax.dot_general(
                    queries[r, rows, :],
                    keys,
                    (((1,), (1,)), ((), ())),
                    preferred_element_type=jnp.float32,
                ) * (0.5 * SCALE)

            @pl.when(plain)
            def _():
                bias = 0.5 * biases[gap_low]
                for part in range(2):
                    rows, half = scores(part)
                    half = half + bias
                    weights = (half + half * jnp.tanh(half)).astype(jnp.bfloat16)
                    acc[rows, :] += jnp.dot(weights, values, preferred_element_type=jnp.float32)

            @pl.when(jnp.logical_not(plain))
            def _():
                k_row = k_ids[ky, pl.ds(zl_from, 1), :]
                column = lax.broadcasted_iota(jnp.int32, (1, PAIR), 1)
                k_pos = k_first + ((column >> 7) ^ core) * BLOCK + (column & (RUN - 1))
                for part in range(2):
                    rows, half = scores(part)
                    gaps = jnp.clip(q_ids[r, rows, :] - k_row, 0, NB - 1)
                    bias = jnp.concatenate(
                        [
                            jnp.take_along_axis(
                                table_rows,
                                gaps[:, c * DH : (c + 1) * DH],
                                axis=1,
                                mode="promise_in_bounds",
                            )
                            for c in range(PAIR // DH)
                        ],
                        axis=1,
                    )
                    half = half + 0.5 * bias
                    q_pos = first + part * PAIR + lax.broadcasted_iota(jnp.int32, (PAIR, 1), 0)
                    seen = (k_pos <= q_pos) & (k_pos >= user_start(q_pos))
                    silu = half + half * jnp.tanh(half)
                    weights = jnp.where(seen, silu, 0.0).astype(jnp.bfloat16)
                    acc[rows, :] += jnp.dot(weights, values, preferred_element_type=jnp.float32)

            return carry

        lowest = jnp.maximum((start_low - (BLOCK + RUN - 1) - zh * RUN + 1023) >> 10, 0)
        lax.fori_loop(lowest, group * 2 + zl + 1, tile, 0)
        attended = acc[...]
        centered = attended - jnp.mean(attended, axis=-1, keepdims=True)
        for zh_to in range(4):
            rows = slice(zh_to * RUN, (zh_to + 1) * RUN)
            send_ref[group * 4 + zh_to] = centered[rows, :].astype(jnp.bfloat16)


def finish_kernel(place, parts, u0, u1, u2, u3, gain, weights, own_ref, send_ref, gated):
    y, x = place[0], place[4]
    for k, u in enumerate((u0, u1, u2, u3)):
        head = (y + k) & 3
        attended = parts[head * 4].astype(jnp.float32)
        for part in range(1, 4):
            attended += parts[head * 4 + part].astype(jnp.float32)
        mean = jnp.mean(attended, axis=-1, keepdims=True)
        centered = attended - mean
        var = jnp.mean(centered * centered, axis=-1, keepdims=True)
        normed = centered * lax.rsqrt(var + NORM_EPS) * gain[pl.ds(head, 1), :]
        columns = pl.ds(pl.multiple_of(head * DH, DH), DH)
        gated[:, columns] = (normed * u[...].astype(jnp.float32)).astype(jnp.bfloat16)
    for k in range(4):
        ky = (y - x - k) & 3
        for m in range(4):
            columns = slice(m * 256, (m + 1) * 256)
            right = jnp.concatenate([weights[j * 4 + m, ky] for j in range(4)], axis=0)
            part = lax.dot_general(
                gated[...], right, (((1,), (1,)), ((), ())), preferred_element_type=jnp.float32
            )
            if k == 0:
                own_ref[:, columns] = part
            else:
                send_ref[k - 1, :, columns] = part.astype(jnp.bfloat16)


def add_kernel(tokens, own, p1, p2, p3, out_ref):
    total = tokens[...].astype(jnp.float32) + own[...]
    for part in (p1, p2, p3):
        total += part[...].astype(jnp.float32)
    out_ref[...] = total.astype(jnp.bfloat16)


def call(kernel, shapes, n_smem, n_vmem, scratch, flops, moved, vmem, name):
    return pl.pallas_call(
        kernel,
        out_shape=shapes,
        in_specs=[pl.BlockSpec(memory_space=pltpu.SMEM)] * n_smem
        + [pl.BlockSpec(memory_space=pltpu.VMEM)] * n_vmem,
        out_specs=jax.tree.map(lambda _: pl.BlockSpec(memory_space=pltpu.VMEM), shapes),
        scratch_shapes=scratch,
        compiler_params=pltpu.CompilerParams(vmem_limit_bytes=vmem * 2**20),
        cost_estimate=pl.CostEstimate(flops=flops, bytes_accessed=moved, transcendentals=0),
        name=name,
    )


def on_device(tokens, w_uvqk, w_out, rab_table, norm_gain, user_lengths, bucket_ids):
    bf16, f32 = jnp.bfloat16, jnp.float32
    y, zl, core, zh, x = (lax.axis_index(a) for a in ("y", "zl", "core", "zh", "x"))
    place = jnp.stack([y, zl, core, zh, x]).astype(jnp.int32)
    plane = ("zh", "zl", "core")

    ids = jnp.stack([bucket_ids // 128, bucket_ids % 128]).astype(bf16)
    ids = jnp.concatenate([ids, jnp.zeros((14, BLOCK), bf16)], axis=0)

    def columns(owner):
        part = lax.dynamic_slice_in_dim(w_uvqk, owner * 512, 512, 1)
        return jnp.concatenate([part, ids], axis=0)

    pieces = [columns(y)] + [
        lax.ppermute(columns((y + k) & 3), "y", [(i, (i + k) % 4) for i in range(4)])
        for k in range(1, 4)
    ]
    piece = jnp.stack(pieces)
    weights = lax.all_gather(piece, plane)

    travelling, _ = lax.optimization_barrier((tokens, piece))

    first = rotations(jnp.concatenate([travelling[:, :512], w_out.T], axis=0), "y", 4)
    second = rotations(travelling[:, 512:], "x", 4)
    first, second = lax.optimization_barrier((first, second))
    firsts = rotations(jnp.concatenate([f[:RUN] for f in first], axis=0), "x", 4)
    seconds = rotations(jnp.concatenate(second, axis=0), "y", 4)
    wo_rows = jnp.stack([f[RUN:] for f in first])
    firsts, seconds, wo_rows = lax.optimization_barrier((firsts, seconds, wo_rows))

    def project(place, low, shapes, name):
        return call(
            functools.partial(project_kernel, low),
            shapes,
            1,
            9,
            [pltpu.VMEM((512, 256), f32)],
            512 * 512 * 4096,
            9 * 2**20,
            20,
            name,
        )(place, *firsts, *seconds, weights)

    (kv,) = project(place, DH, [jax.ShapeDtypeStruct((4, RUN, 2 * DH), bf16)], "project_kv")
    after, kv = lax.optimization_barrier((place, kv))
    u, q = project(after, 0, [jax.ShapeDtypeStruct((4, RUN, DH), bf16)] * 2, "project_uq")

    wo_rows, _ = lax.optimization_barrier((wo_rows, weights))
    wo_all = lax.all_gather(wo_rows, plane)

    from_zl, q = lax.optimization_barrier((swap(kv, "zl"), q))
    kv_near = jnp.stack([kv, from_zl])
    kv_far = swap(kv_near, "core")
    q_all = rotations(q, "zh", 4)

    coded = weights[:4, :, 64:66].astype(f32)
    all_ids = (coded[:, :, 0] * 128 + coded[:, :, 1]).astype(jnp.int32).transpose(1, 0, 2)
    q_ids = lax.dynamic_slice(all_ids, (0, zl * 2 + core, 0), (4, 1, BLOCK)).reshape(4, BLOCK, 1)
    q_edges = jnp.concatenate([q_ids[:, 0], q_ids[:, -1]], axis=1)
    k_ids = lax.dynamic_slice(all_ids, (0, 0, zh * RUN), (4, 4, RUN))
    k_edges = jnp.stack([k_ids[:, ::2, 0], k_ids[:, 1::2, -1]], axis=-1).reshape(4, 4)
    k_ids = k_ids.reshape(4, 2, 2, RUN)
    k_ids = jnp.where(core == 0, k_ids, k_ids[:, :, ::-1]).reshape(4, 2, PAIR)
    biases = lax.dynamic_slice(rab_table, (x * 4 + y, 0), (1, NB))
    gains = lax.dynamic_slice(norm_gain, (x * 4, 0), (4, DH))
    table = jnp.pad(biases, ((0, 0), (0, DH - NB)))

    parts = call(
        attend_kernel,
        jax.ShapeDtypeStruct((16, RUN, DH), bf16),
        5,
        9,
        [pltpu.VMEM((4, BLOCK, DH), bf16), pltpu.VMEM((BLOCK, DH), f32)],
        4 * 512 * 4096 * DH,
        5 * 2**20,
        14,
        "attend",
    )(place, user_lengths, q_edges, k_edges, biases[0], *q_all, kv_near, kv_far, q_ids, k_ids, table)

    u, _ = lax.optimization_barrier((u, (kv_far, q_all)))
    u_own = [u[0]] + [
        lax.ppermute(u[k], "y", [(i, (i - k) % 4) for i in range(4)]) for k in range(1, 4)
    ]
    arrived = lax.all_to_all(parts, ("y", "zh"), 0, 0, tiled=True)
    arrived, wo_all = lax.optimization_barrier((arrived, wo_all))
    own, shares = call(
        finish_kernel,
        [jax.ShapeDtypeStruct((RUN, 1024), f32), jax.ShapeDtypeStruct((3, RUN, 1024), bf16)],
        1,
        7,
        [pltpu.VMEM((RUN, 4 * DH), bf16)],
        2 * RUN * 512 * 4096,
        5 * 2**20,
        14,
        "finish",
    )(place, arrived, *u_own, gains, wo_all)
    shares = [
        lax.ppermute(shares[k - 1], "x", [(i, (i + k) % 4) for i in range(4)]) for k in range(1, 4)
    ]
    return call(
        add_kernel,
        jax.ShapeDtypeStruct((RUN, 1024), bf16),
        0,
        5,
        [],
        5 * RUN * 1024,
        2**20,
        8,
        "add",
    )(tokens, own, *shares)


def solution(mesh):
    fine = Mesh(mesh.devices.reshape(4, 2, 2, 4, 4), ("y", "zl", "core", "zh", "x"))
    every = ("y", "zl", "core", "zh")
    placed = (
        P(every, "x"),
        P(every, "x"),
        P("x", every),
        P(),
        P(),
        P(),
        P(("y", "zl", "core")),
    )
    return jax.shard_map(
        on_device, mesh=fine, in_specs=placed, out_specs=P(every, "x"), check_vma=False
    )
```
